32 devices in a mesh: inp: 8 (over y, x, core), tf: 4 (over z).
Axes of the slice: x: 2, y: 2, z: 4, core: 2. Of those that a mesh axis runs over, the one named last changes fastest.
Arguments:
- voltages: bfloat16 [2, 2048, 16384], P(None, 'inp', 'tf'), may hold values from -6 to 6
- window: float32 [4, 128], replicated, may hold values from -3 to 3
Outputs:
- visibilities: float32 [128, 2, 2048, 1280], P('tf', None, 'inp')
The draws below stay inside these ranges and needn't reach their ends.
All inputs are finite; a program needn't handle non-finite values.
Results may differ from the reference program's by a relative error of at most 0.0034.
Values may be sent and summed in bfloat16 or wider, within the bound.
No kernel may reach another device: no remote copies, remote signals or barrier semaphores. Data moves between devices by JAX's collectives and lax.ppermute only.
A program may use at most 320 MiB of HBM per device.

```python
import math
import jax
import jax.numpy as jnp
from jax import lax

INPUTS = 2048
CHANNELS = 128
TAPS = 4
SPECTRA = 128
SAMPLES = 16384
BLOCK = 256
SLOTS = 1280
N_INP = 8


def levels(stream_key, shape, split, smallest, high):
    factor_of = 1.0
    for dim, parts in split:
        draws = jax.random.uniform(jax.random.fold_in(jax.random.fold_in(stream_key, 6), dim), (parts,), jnp.float32, smallest / len(split), high / len(split))
        factor_of = factor_of * jnp.repeat(jnp.exp(draws), shape[dim] // parts).reshape((-1,) + (1,) * (len(shape) - 1 - dim))
    return factor_of


def noise(key, dims, scale, most, shards=(), kind=jnp.bfloat16):
    gain = levels(key, dims, shards, -0.22, 0.18) if shards else 1.0
    array = jax.random.normal(key, dims, jnp.float32) * scale * gain
    return jnp.minimum(jnp.maximum(array, -most), most).astype(kind)


def setup_inputs(seed: int = 0) -> dict:
    key_list = jax.random.split(jax.random.key(seed), 3)
    voltages = noise(key_list[0], (2, INPUTS, SAMPLES), 1.0, 6.0, ((1, 8), (2, 4)))
    window = noise(key_list[1], (TAPS, CHANNELS), 0.5, 3.0, (), jnp.float32)
    return {"voltages": voltages, "window": window}


def reference(voltages, window):

    def channelize(group_volts):
        frames = group_volts.astype(jnp.float32).reshape(2, BLOCK, SPECTRA, CHANNELS)
        padded = jnp.concatenate([frames, jnp.zeros((2, BLOCK, TAPS - 1, CHANNELS), jnp.float32)], axis=2)
        filtered = jnp.zeros((2, BLOCK, SPECTRA, CHANNELS), jnp.float32)
        for tap_index in range(TAPS):
            filtered = filtered + window[tap_index] * padded[:, :, tap_index:tap_index + SPECTRA]
        transformed = jnp.fft.fft(lax.complex(filtered[0], filtered[1]), axis=-1) / math.sqrt(CHANNELS)
        return jnp.stack([jnp.real(transformed), jnp.imag(transformed)]).astype(jnp.bfloat16)
    grouped = voltages.reshape(2, N_INP, BLOCK, SAMPLES).transpose(1, 0, 2, 3)
    channelized = lax.map(channelize, grouped)
    by_channel = channelized.transpose(4, 1, 0, 2, 3).reshape(CHANNELS, 2, INPUTS, SPECTRA)
    slot_ids = jnp.arange(SLOTS, dtype=jnp.int32)
    block_ids = jnp.arange(N_INP, dtype=jnp.int32)
    partner = (block_ids[:, None] + slot_ids[None, :] // BLOCK) % N_INP * BLOCK + slot_ids[None, :] % BLOCK
    scale = 1.0 / math.sqrt(SPECTRA)

    def correlate(channel):
        values = channel.astype(jnp.float32)
        rows = values.reshape(2, N_INP, BLOCK, SPECTRA)
        partners = values[:, partner]
        real_part = jnp.einsum('pnas,pnbs->nab', rows, partners)
        imag_part = jnp.einsum('nas,nbs->nab', rows[1], partners[0]) - jnp.einsum('nas,nbs->nab', rows[0], partners[1])
        return (jnp.stack([real_part, imag_part]) * scale).reshape(2, INPUTS, SLOTS)
    return lax.map(correlate, by_channel)
```

```python
import functools
import math

import jax
import jax.numpy as jnp
import numpy as np
from jax import lax
from jax.experimental import pallas as pl
from jax.experimental.pallas import tpu as pltpu
from jax.sharding import PartitionSpec as P

GROUP = 4


def dft_tables(length):
    indices = np.arange(length)
    phase = 2.0 * np.pi / length * (indices[:, None] * indices[None, :] % length)
    cosine = np.cos(phase) / math.sqrt(length)
    sine = np.sin(phase) / math.sqrt(length)
    upper = np.concatenate([cosine, sine], axis=1)
    lower = np.concatenate([-sine, cosine], axis=1)
    table = np.concatenate([upper, lower], axis=0).astype(np.float32)
    high = table.astype(jnp.bfloat16)
    low = (table - high.astype(np.float32)).astype(jnp.bfloat16)
    return np.stack([high, low])


def spectra_kernel(place, groups, kept, chunks, merge, *refs):
    refs = list(refs)
    me_ref = refs.pop(0)
    here, after = refs.pop(0), refs.pop(0)
    halo = refs.pop(0) if place["halo"] else None
    window, table = refs.pop(0), refs.pop(0)
    earlier = refs.pop(0) if merge else None
    store = refs.pop()
    own_ref = refs.pop(0)
    outs = refs
    step = pl.program_id(0)
    channels = window.shape[1]
    taps = window.shape[0]
    inputs = here.shape[1]
    frames = groups * GROUP
    rows = 2 * frames
    lane_tiles = inputs // 128

    def run(tail):
        weights = [window[t : t + 1, :] for t in range(taps)]
        filtered = []
        for part in range(2):
            loaded = [here[part, :, i * channels : (i + 1) * channels] for i in range(GROUP)]
            loaded += [tail[part, :, i * channels : (i + 1) * channels] for i in range(taps - 1)]
            loaded = [x.astype(jnp.float32) for x in loaded]
            filtered.append(
                [sum(weights[t] * loaded[i + t] for t in range(taps)) for i in range(GROUP)]
            )
        for i in range(GROUP):
            both = jnp.concatenate([filtered[0][i], filtered[1][i]], axis=1)
            high = both.astype(jnp.bfloat16)
            low = (both - high.astype(jnp.float32)).astype(jnp.bfloat16)
            nt = functools.partial(
                lax.dot_general,
                dimension_numbers=(((1,), (1,)), ((), ())),
                preferred_element_type=jnp.float32,
            )
            out = nt(table[0], high) + (nt(table[1], high) + nt(table[0], low))
            for part in range(2):
                first = part * frames + step * GROUP + i
                for lane in range(lane_tiles):
                    store[lane, pl.ds(first, channels, stride=rows), :] = out[
                        part * channels : (part + 1) * channels, lane * 128 : (lane + 1) * 128
                    ]

    if halo is None:
        run(after)
    else:
        last = pl.num_programs(0) - 1

        @pl.when(step < last)
        def _():
            run(after)

        @pl.when(step == last)
        def _():
            run(halo)

    @pl.when(step == pl.num_programs(0) - 1)
    def _():
        devices = channels // kept

        def piece(channel):
            start = pl.multiple_of(channel * rows, rows)
            got = [store[lane, pl.ds(start, rows), :] for lane in range(lane_tiles)]
            return jnp.concatenate(got, axis=1).astype(jnp.bfloat16)

        me = me_ref[0]

        def own(i, carry):
            own_ref[i] = piece(me * kept + i)
            return carry

        lax.fori_loop(0, kept, own, 0)
        for hop in range(1, devices):
            base = lax.rem(me + hop, devices) * kept
            if merge:
                first = 0
                for q, size in enumerate(chunks):
                    out = outs[(hop - 1) * len(chunks) + q]

                    def one(i, carry, out=out, first=first, base=base, hop=hop):
                        out[i, :rows, :] = earlier[hop - 1, first + i]
                        out[i, rows:, :] = piece(base + first + i)
                        return carry

                    lax.fori_loop(0, size, one, 0)
                    first += size
            else:

                def rest(i, carry, base=base, hop=hop):
                    outs[0][hop - 1, i] = piece(base + i)
                    return carry

                lax.fori_loop(0, kept, rest, 0)


def spectra_part(voltages, halo, window, table, me, devices, first, groups, chunks, earlier):
    parts, inputs, samples = voltages.shape
    channels = window.shape[1]
    kept = channels // devices
    rows = 2 * groups * GROUP
    width = GROUP * channels
    last = samples // width - 1
    merge = earlier is not None
    operands = [me, voltages, voltages]
    in_specs = [
        pl.BlockSpec(memory_space=pltpu.SMEM),
        pl.BlockSpec((2, inputs, width), lambda i: (0, 0, first + i)),
        pl.BlockSpec((2, inputs, width), lambda i: (0, 0, jnp.minimum(first + i + 1, last))),
    ]
    whole = lambda shape: pl.BlockSpec(shape, lambda i: (0,) * len(shape))
    if halo is not None:
        operands.append(halo)
        in_specs.append(whole(halo.shape))
    operands += [window, table]
    in_specs += [whole(window.shape), whole(table.shape)]
    shapes = [(kept, rows, inputs)]
    if merge:
        operands.append(earlier)
        in_specs.append(whole(earlier.shape))
        shapes += [(size, 2 * rows, inputs) for _ in range(devices - 1) for size in chunks]
    else:
        shapes.append((devices - 1, kept, rows, inputs))
    return pl.pallas_call(
        functools.partial(
            spectra_kernel, {"halo": halo is not None}, groups, kept, chunks, merge
        ),
        grid=(groups,),
        out_shape=[jax.ShapeDtypeStruct(s, jnp.bfloat16) for s in shapes],
        in_specs=in_specs,
        out_specs=[whole(s) for s in shapes],
        scratch_shapes=[pltpu.VMEM((inputs // 128, channels * rows, 128), jnp.float32)],
        compiler_params=pltpu.CompilerParams(
            vmem_limit_bytes=48 * 1024 * 1024, dimension_semantics=("arbitrary",)
        ),
        cost_estimate=pl.CostEstimate(
            flops=2 * 3 * 4 * channels * channels * inputs * groups * GROUP,
            bytes_accessed=2 * voltages.size,
            transcendentals=0,
        ),
    )(*operands)


def pairs_kernel(scale, half, count, counts, *refs):
    out = refs[-1]
    per_block = [refs[n * count : (n + 1) * count] for n in range(half + 1)]

    def pieces(block):
        got = []
        for ref, many in zip(per_block[block], counts):
            values = [ref[0]] if many is None else [ref[m, 0] for m in range(many)]
            for value in values:
                got.append(value)
        return got

    mine = pieces(0)
    turned = []
    for value in mine:
        size = 2 * PART_FRAMES
        for first in range(0, value.shape[0], size):
            turned.append(value[first + PART_FRAMES : first + size])
            turned.append(-value[first : first + PART_FRAMES])
    left = jnp.concatenate(mine, axis=0).T
    left_turned = jnp.concatenate(turned, axis=0).T
    width = left.shape[0]
    for block in range(half + 1):
        right = jnp.concatenate(pieces(block), axis=0)
        columns = slice(block * width, (block + 1) * width)
        out[0, 0, :, columns] = (
            jnp.dot(left, right, preferred_element_type=jnp.float32) * scale
        )
        out[0, 1, :, columns] = (
            jnp.dot(left_turned, right, preferred_element_type=jnp.float32) * scale
        )


PART_FRAMES = 16


def pairs(blocks, total, first, size, kept, scale):
    half = len(blocks) - 1
    inputs = blocks[0][0][0].shape[-1]
    operands, in_specs, counts = [], [], []
    depth = 0
    for number, block in enumerate(blocks):
        for array, stack, offset in block:
            operands.append(array)
            if array.ndim - (stack is not None) == 3:
                rows = array.shape[-2]
                if number == 0:
                    counts.append(None)
                    depth += rows
                if stack is None:
                    spec = pl.BlockSpec((1, rows, inputs), lambda i, o=offset: (o + i, 0, 0))
                else:
                    spec = pl.BlockSpec(
                        (None, 1, rows, inputs), lambda i, o=offset, s=stack: (s, o + i, 0, 0)
                    )
            else:
                many, rows = array.shape[-4], array.shape[-2]
                if number == 0:
                    counts.append(many)
                    depth += many * rows
                if stack is None:
                    spec = pl.BlockSpec(
                        (many, 1, rows, inputs), lambda i, o=offset: (0, o + i, 0, 0)
                    )
                else:
                    spec = pl.BlockSpec(
                        (None, many, 1, rows, inputs),
                        lambda i, o=offset, s=stack: (s, 0, o + i, 0, 0),
                    )
            in_specs.append(spec)
    count = len(counts)
    slots = (half + 1) * inputs
    aliases = {}
    if total is not None:
        aliases = {len(operands): 0}
        operands.append(total)
        in_specs.append(pl.BlockSpec(memory_space=pl.ANY))

    def body(*refs):
        refs = list(refs)
        if total is not None:
            refs.pop(-2)
        pairs_kernel(scale, half, count, counts, *refs)

    return pl.pallas_call(
        body,
        grid=(size,),
        out_shape=jax.ShapeDtypeStruct((kept, 2, inputs, slots), jnp.float32),
        in_specs=in_specs,
        out_specs=pl.BlockSpec((1, 2, inputs, slots), lambda i: (first + i, 0, 0, 0)),
        input_output_aliases=aliases,
        compiler_params=pltpu.CompilerParams(
            vmem_limit_bytes=32 * 1024 * 1024, dimension_semantics=("arbitrary",)
        ),
        cost_estimate=pl.CostEstimate(
            flops=2 * size * 2 * inputs * slots * depth,
            bytes_accessed=size * 2 * inputs * slots * 4,
            transcendentals=0,
        ),
    )(*operands)


def shifted(x, axis, by):
    devices = lax.axis_size(axis)
    return lax.ppermute(x, axis, [(i, (i + by) % devices) for i in range(devices)])


def swapped(x, axis, bit):
    devices = lax.axis_size(axis)
    return lax.ppermute(x, axis, [(i, i ^ bit) for i in range(devices)])


def partners(own, axis):
    devices = lax.axis_size(axis)
    if devices != 8:
        return [(shifted(own, axis, -hop), None) for hop in range(1, devices // 2 + 1)]
    place = lax.axis_index(axis)
    is_far = (place & 2) == 2
    is_odd = (place & 1) == 1
    over_y = swapped(own, axis, 4)
    over_x = swapped(jnp.where(is_far, own, over_y), axis, 2)
    sent = jnp.where(is_odd, jnp.stack([own, over_x]), jnp.stack([over_x, over_y]))
    over_core = swapped(sent, axis, 1)
    return [(over_core, 0), (over_x, None), (over_core, 1), (over_y, None)]


def chunk_sizes(kept):
    if kept < 16:
        return [kept]
    return [kept // 4] * 4


def on_device(voltages, window):
    tap_count, channels = window.shape
    frames_dev = voltages.shape[2] // channels
    devices = lax.axis_size("tf")
    kept = channels // devices
    chunks = chunk_sizes(kept)
    groups = frames_dev // GROUP // 2
    leading = voltages[:, :, : (tap_count - 1) * channels]
    halo = lax.ppermute(leading, "tf", [(i, i - 1) for i in range(1, devices)])
    table = jnp.asarray(dft_tables(channels))
    me = lax.axis_index("tf").astype(jnp.int32).reshape(1)
    own_a, rest = spectra_part(
        voltages, None, window, table, me, devices, 0, groups, chunks, None
    )
    own_b, *pieces = spectra_part(
        voltages, halo, window, table, me, devices, groups, groups, chunks, rest
    )
    scale = 1.0 / math.sqrt(frames_dev * devices)
    first_a = [(own_a, None)] + partners(own_a, "inp")
    first_b = [(own_b, None)] + partners(own_b, "inp")
    total = None
    first = 0
    for q, size in enumerate(chunks):
        arrived = [
            shifted(pieces[(hop - 1) * len(chunks) + q], "tf", hop) for hop in range(1, devices)
        ]
        own = jnp.stack(arrived)
        later = [(own, None)] + partners(own, "inp")
        blocks = [
            [(*a, first), (*b, first), (*c, 0)] for a, b, c in zip(first_a, first_b, later)
        ]
        total = pairs(blocks, total, first, size, kept, scale)
        first += size
    return total


def solution(mesh):
    in_specs = (P(None, "inp", "tf"), P())
    out_specs = P("tf", None, "inp", None)
    return jax.shard_map(
        on_device, mesh=mesh, in_specs=in_specs, out_specs=out_specs, check_vma=False
    )
```

```python
import functools
import math

import jax
import jax.numpy as jnp
import numpy as np
from jax import lax
from jax.experimental import pallas as pl
from jax.experimental.pallas import tpu as pltpu
from jax.sharding import PartitionSpec as P

GROUP = 4
PAD = 8


def dft_tables(length):
    indices = np.arange(length)
    phase = 2.0 * np.pi / length * (indices[:, None] * indices[None, :] % length)
    cosine = np.cos(phase) / math.sqrt(length)
    sine = np.sin(phase) / math.sqrt(length)
    upper = np.concatenate([cosine, sine], axis=1)
    lower = np.concatenate([-sine, cosine], axis=1)
    table = np.concatenate([upper, lower], axis=0).astype(np.float32)
    high = table.astype(jnp.bfloat16)
    low = (table - high.astype(np.float32)).astype(jnp.bfloat16)
    return np.stack([high, low])


def spectra_kernel(place, groups, kept, cuts, merge, *refs):
    refs = list(refs)
    me_ref = refs.pop(0)
    here, after = refs.pop(0), refs.pop(0)
    halo = refs.pop(0) if place["halo"] else None
    window, table = refs.pop(0), refs.pop(0)
    earlier = refs.pop(0) if merge else None
    store = refs.pop()
    own_ref = refs.pop(0)
    outs = refs
    step = pl.program_id(0)
    channels = window.shape[1]
    taps = window.shape[0]
    inputs = here.shape[1]
    frames = groups * GROUP
    rows = 2 * frames
    lane_tiles = inputs // 128

    def run(tail):
        weights = [window[t : t + 1, :] for t in range(taps)]
        filtered = []
        for part in range(2):
            loaded = [here[part, :, i * channels : (i + 1) * channels] for i in range(GROUP)]
            loaded += [tail[part, :, i * channels : (i + 1) * channels] for i in range(taps - 1)]
            loaded = [x.astype(jnp.float32) for x in loaded]
            filtered.append(
                [sum(weights[t] * loaded[i + t] for t in range(taps)) for i in range(GROUP)]
            )
        for i in range(GROUP):
            both = jnp.concatenate([filtered[0][i], filtered[1][i]], axis=1)
            high = both.astype(jnp.bfloat16)
            low = (both - high.astype(jnp.float32)).astype(jnp.bfloat16)
            nt = functools.partial(
                lax.dot_general,
                dimension_numbers=(((1,), (1,)), ((), ())),
                preferred_element_type=jnp.float32,
            )
            out = nt(table[0], high) + (nt(table[1], high) + nt(table[0], low))
            for part in range(2):
                first = part * frames + step * GROUP + i
                for lane in range(lane_tiles):
                    store[lane, pl.ds(first, channels, stride=rows + PAD), :] = out[
                        part * channels : (part + 1) * channels, lane * 128 : (lane + 1) * 128
                    ]

    if halo is None:
        run(after)
    else:
        last = pl.num_programs(0) - 1

        @pl.when(step < last)
        def _():
            run(after)

        @pl.when(step == last)
        def _():
            run(halo)

    @pl.when(step == pl.num_programs(0) - 1)
    def _():
        devices = channels // kept

        def piece(channel):
            start = pl.multiple_of(channel * (rows + PAD), 8)
            got = [store[lane, pl.ds(start, rows), :] for lane in range(lane_tiles)]
            return jnp.concatenate(got, axis=1).astype(jnp.bfloat16)

        me = me_ref[0]

        def own(i, carry):
            own_ref[i] = piece(me * kept + i)
            return carry

        lax.fori_loop(0, kept, own, 0, unroll=2)
        for number, cut in enumerate(cuts):
            at = 0
            for hop, first, size in cut:
                base = (me ^ hop) * kept + first

                def one(i, carry, out=outs[number], at=at, base=base, hop=hop, first=first):
                    if merge:
                        out[at + i, :rows, :] = earlier[hop - 1, first + i]
                        out[at + i, rows:, :] = piece(base + i)
                    else:
                        out[at + i] = piece(base + i)
                    return carry

                lax.fori_loop(0, size, one, 0, unroll=2)
                at += size


def spectra_part(voltages, halo, window, table, me, devices, first, groups, cuts, earlier):
    parts, inputs, samples = voltages.shape
    channels = window.shape[1]
    kept = channels // devices
    rows = 2 * groups * GROUP
    width = GROUP * channels
    last = samples // width - 1
    merge = earlier is not None
    operands = [me, voltages, voltages]
    in_specs = [
        pl.BlockSpec(memory_space=pltpu.SMEM),
        pl.BlockSpec((2, inputs, width), lambda i: (0, 0, first + i)),
        pl.BlockSpec((2, inputs, width), lambda i: (0, 0, jnp.minimum(first + i + 1, last))),
    ]
    whole = lambda shape: pl.BlockSpec(shape, lambda i: (0,) * len(shape))
    if halo is not None:
        operands.append(halo)
        in_specs.append(whole(halo.shape))
    operands += [window, table]
    in_specs += [whole(window.shape), whole(table.shape)]
    shapes = [(kept, rows, inputs)]
    if merge:
        operands.append(earlier)
        in_specs.append(whole(earlier.shape))
    depth = 2 * rows if merge else rows
    shapes += [(sum(size for _, _, size in cut), depth, inputs) for cut in cuts]
    return pl.pallas_call(
        functools.partial(
            spectra_kernel, {"halo": halo is not None}, groups, kept, cuts, merge
        ),
        grid=(groups,),
        out_shape=[jax.ShapeDtypeStruct(s, jnp.bfloat16) for s in shapes],
        in_specs=in_specs,
        out_specs=[whole(s) for s in shapes],
        scratch_shapes=[pltpu.VMEM((inputs // 128, channels * (rows + PAD), 128), jnp.float32)],
        compiler_params=pltpu.CompilerParams(
            vmem_limit_bytes=48 * 1024 * 1024, dimension_semantics=("arbitrary",)
        ),
        cost_estimate=pl.CostEstimate(
            flops=2 * 3 * 4 * channels * channels * inputs * groups * GROUP,
            bytes_accessed=2 * voltages.size,
            transcendentals=0,
        ),
    )(*operands)


def pairs_kernel(scale, half, count, step, *refs):
    out = refs[-1]
    per_block = [refs[n * count : (n + 1) * count] for n in range(half + 1)]
    for channel in range(step):

        def pieces(block):
            got = []
            for ref in per_block[block]:
                if ref.ndim == 3:
                    got.append(ref[channel])
                else:
                    got += [ref[m, channel] for m in range(ref.shape[0])]
            return got

        mine = pieces(0)
        turned = []
        for value in mine:
            size = 2 * PART_FRAMES
            for first in range(0, value.shape[0], size):
                turned.append(value[first + PART_FRAMES : first + size])
                turned.append(-value[first : first + PART_FRAMES])
        left = jnp.concatenate(mine, axis=0).T
        left_turned = jnp.concatenate(turned, axis=0).T
        width = left.shape[0]
        for block in range(half + 1):
            right = jnp.concatenate(pieces(block), axis=0)
            columns = slice(block * width, (block + 1) * width)
            out[channel, 0, :, columns] = (
                jnp.dot(left, right, preferred_element_type=jnp.float32) * scale
            )
            out[channel, 1, :, columns] = (
                jnp.dot(left_turned, right, preferred_element_type=jnp.float32) * scale
            )


PART_FRAMES = 16


def pairs(blocks, total, first, size, kept, scale):
    half = len(blocks) - 1
    inputs = blocks[0][0][0].shape[-1]
    operands, in_specs = [], []
    count = len(blocks[0])
    offsets = [offset for block in blocks for _, _, offset in block]
    step = 2 if all(x % 2 == 0 for x in [size, first, *offsets]) else 1
    for block in blocks:
        for array, stack, offset in block:
            operands.append(array)
            rows = array.shape[-2]
            at = offset // step
            lead = array.shape[:-3] if stack is None else array.shape[1:-3]
            zeros = (0,) * len(lead)
            if stack is None:
                shape, index = (*lead, step, rows, inputs), lambda i, a=at, z=zeros: (*z, a + i, 0, 0)
            else:
                shape = (None, *lead, step, rows, inputs)
                index = lambda i, a=at, s=stack, z=zeros: (s, *z, a + i, 0, 0)
            in_specs.append(pl.BlockSpec(shape, index))
    depth = sum(math.prod(x.shape[:-3] if st is None else x.shape[1:-3]) * x.shape[-2] for x, st, _ in blocks[0])
    slots = (half + 1) * inputs
    aliases = {}
    if total is not None:
        aliases = {len(operands): 0}
        operands.append(total)
        in_specs.append(pl.BlockSpec(memory_space=pl.ANY))

    def body(*refs):
        refs = list(refs)
        if total is not None:
            refs.pop(-2)
        pairs_kernel(scale, half, count, step, *refs)

    return pl.pallas_call(
        body,
        grid=(size // step,),
        out_shape=jax.ShapeDtypeStruct((kept, 2, inputs, slots), jnp.float32),
        in_specs=in_specs,
        out_specs=pl.BlockSpec((step, 2, inputs, slots), lambda i: (first // step + i, 0, 0, 0)),
        input_output_aliases=aliases,
        compiler_params=pltpu.CompilerParams(
            vmem_limit_bytes=32 * 1024 * 1024, dimension_semantics=("arbitrary",)
        ),
        cost_estimate=pl.CostEstimate(
            flops=2 * size * 2 * inputs * slots * depth,
            bytes_accessed=size * 2 * inputs * slots * 4,
            transcendentals=0,
        ),
    )(*operands)


def shifted(x, axis, by):
    devices = lax.axis_size(axis)
    return lax.ppermute(x, axis, [(i, (i + by) % devices) for i in range(devices)])


def swapped(x, axis, bit):
    devices = lax.axis_size(axis)
    return lax.ppermute(x, axis, [(i, i ^ bit) for i in range(devices)])


def after(x, *earlier):
    return lax.optimization_barrier((x, *earlier))[0]


def partners(own, axis):
    devices = lax.axis_size(axis)
    return [(own, None)] + [(shifted(own, axis, -hop), None) for hop in range(1, devices // 2 + 1)]


def tick(x, *earlier):
    x = lax.optimization_barrier((x, *earlier))[0]

    def body(x_ref, out_ref):
        out_ref[...] = x_ref[...] + 1.0

    return pl.pallas_call(
        body,
        out_shape=jax.ShapeDtypeStruct(x.shape, x.dtype),
        cost_estimate=pl.CostEstimate(
            flops=10**15, bytes_accessed=2 * x.size * 4, transcendentals=0
        ),
    )(x)


def after(x, *earlier):
    return lax.optimization_barrier((x, *earlier))[0]


class Exchange:
    def __init__(self, own, axis):
        self.own, self.axis = own, axis
        place = lax.axis_index(axis)
        self.is_far = (place & 2) == 2
        self.is_odd = (place & 1) == 1

    def y(self, *earlier):
        self.over_y = swapped(after(self.own, *earlier), self.axis, 4)

    def x(self, *earlier):
        own, over_y = lax.optimization_barrier((self.own, self.over_y, *earlier))[:2]
        self.over_x = swapped(jnp.where(self.is_far, own, over_y), self.axis, 2)

    def for_core(self, *earlier):
        own, over_x, over_y = lax.optimization_barrier(
            (self.own, self.over_x, self.over_y, *earlier)
        )[:3]
        return [jnp.where(self.is_odd, own, over_x), jnp.where(self.is_odd, over_x, over_y)]

    def core(self, *earlier):
        sent = jnp.stack(self.for_core(*earlier))
        self.over_core, self.slots = swapped(sent, self.axis, 1), (0, 1)

    def blocks(self):
        return [
            (self.own, None),
            (self.over_core, self.slots[0]),
            (self.over_x, None),
            (self.over_core, self.slots[1]),
            (self.over_y, None),
        ]


def core_of_both(a, b, *earlier):
    sent = jnp.stack(a.for_core(*earlier) + b.for_core(*earlier))
    a.over_core = b.over_core = swapped(sent, a.axis, 1)
    a.slots, b.slots = (0, 1), (2, 3)


def on_device(voltages, window):
    tap_count, channels = window.shape
    frames_dev = voltages.shape[2] // channels
    devices = lax.axis_size("tf")
    kept = channels // devices
    planned = devices == 4 and lax.axis_size("inp") == 8 and kept == 32
    sizes = [6, 6, 6, 6, 4, 4] if planned else [kept]
    nears = [12, 12, 8] if planned else [kept]
    count = len(sizes)
    firsts = [sum(sizes[:q]) for q in range(count)]
    near_firsts = [sum(nears[:h]) for h in range(len(nears))]
    cuts = [[(1, first, size)] for first, size in zip(near_firsts, nears)]
    for hop in range(2, devices):
        cuts += [[(hop, first, size)] for first, size in zip(firsts, sizes)]
    rest_cuts = [[(hop, 0, kept) for hop in range(1, devices)]]
    groups = frames_dev // GROUP // 2
    leading = voltages[:, :, : (tap_count - 1) * channels]
    halo = lax.ppermute(leading, "tf", [(i, i - 1) for i in range(1, devices)])
    table = jnp.asarray(dft_tables(channels))
    me = lax.axis_index("tf").astype(jnp.int32).reshape(1)
    own_a, rest = spectra_part(
        voltages, None, window, table, me, devices, 0, groups, rest_cuts, None
    )
    rest = rest.reshape(devices - 1, kept, *rest.shape[1:])
    own_b, *pieces = spectra_part(
        voltages, halo, window, table, me, devices, groups, groups, cuts, rest
    )
    near = pieces[: len(nears)]
    far = [pieces[len(nears) + q :: count] for q in range(count)]
    scale = 1.0 / math.sqrt(frames_dev * devices)

    def run_pairs(total, q, *groups_):
        blocks = [
            [(*entry, at) for entry, (_, at) in zip(entries, groups_)]
            for entries in zip(*[g for g, _ in groups_])
        ]
        return pairs(blocks, total, firsts[q], sizes[q], kept, scale)

    if not planned:
        near = swapped(near[0], "tf", 1)
        far = jnp.stack([swapped(x, "tf", hop + 2) for hop, x in enumerate(far[0])])
        return run_pairs(None, 0, *[(partners(x, "inp"), 0) for x in (own_a, own_b, near, far)])

    def over_z(q, *earlier):
        sent = lax.optimization_barrier((*far[q], *earlier))
        return [swapped(sent[hop - 2], "tf", hop) for hop in range(2, devices)]

    near_over_z = lambda h, *earlier: swapped(after(near[h], *earlier), "tf", 1)
    exchange = lambda *parts: Exchange(jnp.concatenate(parts), "inp")
    a, b = Exchange(own_a, "inp"), Exchange(own_b, "inp")
    t = jnp.zeros((8, 128), jnp.float32)

    def chunk(q):
        h = max(i for i, first in enumerate(near_firsts) if first <= firsts[q])
        at = nears[q] if q < len(nears) else 0
        return run_pairs(
            total,
            q,
            (a.blocks(), firsts[q]),
            (b.blocks(), firsts[q]),
            (lines[h].blocks(), firsts[q] - near_firsts[h]),
            (lines[q].blocks(), at),
            (lines[q].blocks(), at + sizes[q]),
        )

    total = None
    a.y()
    t = tick(t, own_b[:1, :8, :128])
    z, n, lines = [over_z(0, t)], [near_over_z(0, t)], []
    b.y(t)
    a.x(t)
    t = tick(t, *z[0])
    z.append(over_z(1, t))
    n.append(near_over_z(1, n[0], t))
    lines.append(exchange(n[0], *z[0]))
    lines[0].y(b.over_y, t)
    b.x(a.over_x, t)
    t = tick(t, *z[1], b.over_y, a.over_x)
    z.append(over_z(2, t))
    n.append(near_over_z(2, n[1], t))
    lines.append(exchange(n[1], *z[1]))
    lines[1].y(lines[0].over_y, t)
    lines[0].x(b.over_x, t)
    t = tick(t, *z[2], lines[0].over_y, b.over_x)
    z.append(over_z(3, t))
    lines.append(exchange(n[2], *z[2]))
    lines[2].y(lines[1].over_y, t)
    lines[1].x(lines[0].over_x, t)
    core_of_both(a, b, t)
    t = tick(t, *z[3], lines[1].over_y, lines[0].over_x)
    z.append(over_z(4, t))
    lines.append(exchange(*z[3]))
    lines[3].y(lines[2].over_y, t)
    lines[2].x(lines[1].over_x, t)
    lines[0].core(a.over_core, t)
    t = tick(t, *z[4], lines[2].over_y, lines[1].over_x, a.over_core)
    z.append(over_z(5, t))
    lines.append(exchange(*z[4]))
    lines[4].y(lines[3].over_y, t)
    lines[3].x(lines[2].over_x, t)
    total = chunk(0)
    lines[1].core(lines[0].over_core, t, total)
    t = tick(t, *z[5], lines[3].over_y, lines[2].over_x, lines[0].over_core)
    lines.append(exchange(*z[5]))
    lines[5].y(lines[4].over_y, t)
    lines[4].x(lines[3].over_x, t)
    lines[2].core(lines[1].over_core, t)
    total = chunk(1)
    t = tick(t, lines[4].over_y, lines[3].over_x, lines[1].over_core, total)
    lines[5].x(lines[4].over_x, t)
    lines[3].core(lines[2].over_core, t)
    total = chunk(2)
    t = tick(t, lines[5].over_y, lines[4].over_x, lines[2].over_core, total)
    core_of_both(lines[4], lines[5], t, lines[3].over_core)
    total = chunk(3)
    total = chunk(4)
    total = chunk(5)
    return total


def solution(mesh):
    in_specs = (P(None, "inp", "tf"), P())
    out_specs = P("tf", None, "inp", None)
    return jax.shard_map(
        on_device, mesh=mesh, in_specs=in_specs, out_specs=out_specs, check_vma=False
    )
```

```python
import functools
import math

import jax
import jax.numpy as jnp
import numpy as np
from jax import lax
from jax.experimental import pallas as pl
from jax.experimental.pallas import tpu as pltpu
from jax.sharding import PartitionSpec as P

GROUP = 4
PAD = 8


def dft_tables(length):
    indices = np.arange(length)
    phase = 2.0 * np.pi / length * (indices[:, None] * indices[None, :] % length)
    cosine = np.cos(phase) / math.sqrt(length)
    sine = np.sin(phase) / math.sqrt(length)
    upper = np.concatenate([cosine, sine], axis=1)
    lower = np.concatenate([-sine, cosine], axis=1)
    table = np.concatenate([upper, lower], axis=0).astype(np.float32)
    high = table.astype(jnp.bfloat16)
    low = (table - high.astype(np.float32)).astype(jnp.bfloat16)
    return np.stack([high, low])


def spectra_kernel(place, groups, kept, cuts, merge, *refs):
    refs = list(refs)
    me_ref = refs.pop(0)
    here, after = refs.pop(0), refs.pop(0)
    halo = refs.pop(0) if place["halo"] else None
    window, table = refs.pop(0), refs.pop(0)
    earlier = refs.pop(0) if merge else None
    store = refs.pop()
    own_ref = refs.pop(0)
    outs = refs
    step = pl.program_id(0)
    channels = window.shape[1]
    taps = window.shape[0]
    inputs = here.shape[1]
    frames = groups * GROUP
    rows = 2 * frames
    lane_tiles = inputs // 128

    def run(tail):
        weights = [window[t : t + 1, :] for t in range(taps)]
        filtered = []
        for part in range(2):
            loaded = [here[part, :, i * channels : (i + 1) * channels] for i in range(GROUP)]
            loaded += [tail[part, :, i * channels : (i + 1) * channels] for i in range(taps - 1)]
            loaded = [x.astype(jnp.float32) for x in loaded]
            filtered.append(
                [sum(weights[t] * loaded[i + t] for t in range(taps)) for i in range(GROUP)]
            )
        for i in range(GROUP):
            both = jnp.concatenate([filtered[0][i], filtered[1][i]], axis=1)
            high = both.astype(jnp.bfloat16)
            low = (both - high.astype(jnp.float32)).astype(jnp.bfloat16)
            nt = functools.partial(
                lax.dot_general,
                dimension_numbers=(((1,), (1,)), ((), ())),
                preferred_element_type=jnp.float32,
            )
            out = nt(table[0], high) + (nt(table[1], high) + nt(table[0], low))
            for part in range(2):
                first = part * frames + step * GROUP + i
                for lane in range(lane_tiles):
                    store[lane, pl.ds(first, channels, stride=rows + PAD), :] = out[
                        part * channels : (part + 1) * channels, lane * 128 : (lane + 1) * 128
                    ]

    if halo is None:
        run(after)
    else:
        last = pl.num_programs(0) - 1

        @pl.when(step < last)
        def _():
            run(after)

        @pl.when(step == last)
        def _():
            run(halo)

    @pl.when(step == pl.num_programs(0) - 1)
    def _():
        devices = channels // kept

        def piece(channel):
            start = pl.multiple_of(channel * (rows + PAD), 8)
            got = [store[lane, pl.ds(start, rows), :] for lane in range(lane_tiles)]
            return jnp.concatenate(got, axis=1).astype(jnp.bfloat16)

        me = me_ref[0]

        def own(i, carry):
            own_ref[i] = piece(me * kept + i)
            return carry

        lax.fori_loop(0, kept, own, 0, unroll=2)
        for number, cut in enumerate(cuts):
            at = 0
            for hop, first, size in cut:
                base = (me ^ hop) * kept + first

                def one(i, carry, out=outs[number], at=at, base=base, hop=hop, first=first):
                    if merge:
                        out[at + i, :rows, :] = earlier[hop - 1, first + i]
                        out[at + i, rows:, :] = piece(base + i)
                    else:
                        out[at + i] = piece(base + i)
                    return carry

                lax.fori_loop(0, size, one, 0, unroll=2)
                at += size


def spectra_part(voltages, halo, window, table, me, devices, first, groups, cuts, earlier):
    parts, inputs, samples = voltages.shape
    channels = window.shape[1]
    kept = channels // devices
    rows = 2 * groups * GROUP
    width = GROUP * channels
    last = samples // width - 1
    merge = earlier is not None
    operands = [me, voltages, voltages]
    in_specs = [
        pl.BlockSpec(memory_space=pltpu.SMEM),
        pl.BlockSpec((2, inputs, width), lambda i: (0, 0, first + i)),
        pl.BlockSpec((2, inputs, width), lambda i: (0, 0, jnp.minimum(first + i + 1, last))),
    ]
    whole = lambda shape: pl.BlockSpec(shape, lambda i: (0,) * len(shape))
    if halo is not None:
        operands.append(halo)
        in_specs.append(whole(halo.shape))
    operands += [window, table]
    in_specs += [whole(window.shape), whole(table.shape)]
    shapes = [(kept, rows, inputs)]
    if merge:
        operands.append(earlier)
        in_specs.append(whole(earlier.shape))
    depth = 2 * rows if merge else rows
    shapes += [(sum(size for _, _, size in cut), depth, inputs) for cut in cuts]
    return pl.pallas_call(
        functools.partial(
            spectra_kernel, {"halo": halo is not None}, groups, kept, cuts, merge
        ),
        grid=(groups,),
        out_shape=[jax.ShapeDtypeStruct(s, jnp.bfloat16) for s in shapes],
        in_specs=in_specs,
        out_specs=[whole(s) for s in shapes],
        scratch_shapes=[pltpu.VMEM((inputs // 128, channels * (rows + PAD), 128), jnp.float32)],
        compiler_params=pltpu.CompilerParams(
            vmem_limit_bytes=48 * 1024 * 1024, dimension_semantics=("arbitrary",)
        ),
        cost_estimate=pl.CostEstimate(
            flops=2 * 3 * 4 * channels * channels * inputs * groups * GROUP,
            bytes_accessed=2 * voltages.size,
            transcendentals=0,
        ),
    )(*operands)


def pairs_kernel(scale, count, step, wanted, *refs):
    out, lefts = refs[-2:]
    mine = refs[:count]
    per_block = [refs[n * count : (n + 1) * count] for n in range(1, len(refs) // count)]

    def pieces(block, channel):
        got = []
        for ref in block:
            if len(ref.shape) == 3:
                got.append(ref[channel])
            else:
                got += [ref[m, channel] for m in range(ref.shape[0])]
        return got

    @pl.when(pl.program_id(1) == 0)
    def _():
        for channel in range(step):
            values = pieces(mine, channel)
            turned = []
            for value in values:
                size = 2 * PART_FRAMES
                for first in range(0, value.shape[0], size):
                    turned.append(value[first + PART_FRAMES : first + size])
                    turned.append(-value[first : first + PART_FRAMES])
            lefts[channel, 0] = jnp.concatenate(values, axis=0).T
            lefts[channel, 1] = jnp.concatenate(turned, axis=0).T

    width = lefts.shape[2]
    together = out.shape[-1] // width
    for j in range(len(wanted) // together):

        @pl.when(pl.program_id(1) == j)
        def _(j=j):
            for channel in range(step):
                for k in range(together):
                    right = jnp.concatenate(pieces(per_block[j * together + k], channel), axis=0)
                    for part in range(2):
                        out[channel, part, :, k * width : (k + 1) * width] = (
                            jnp.dot(
                                lefts[channel, part], right, preferred_element_type=jnp.float32
                            )
                            * scale
                        )


PART_FRAMES = 16
NO_COST = pl.CostEstimate(flops=0, bytes_accessed=0, transcendentals=0)


def pairs(blocks, total, first, size, kept, scale, wanted):
    inputs = blocks[0][0][0].shape[-1]
    operands, in_specs = [], []
    count = len(blocks[0])
    used = [blocks[0]] + [blocks[n] for n in wanted]
    offsets = [offset for block in used for _, _, offset in block]
    step = 2 if all(x % 2 == 0 for x in [size, first, *offsets]) else 1
    for block in used:
        for array, stack, offset in block:
            operands.append(array)
            rows = array.shape[-2]
            at = offset // step
            lead = array.shape[:-3] if stack is None else array.shape[1:-3]
            zeros = (0,) * len(lead)
            if stack is None:
                shape = (*lead, step, rows, inputs)
                index = lambda i, j, a=at, z=zeros: (*z, a + i, 0, 0)
            else:
                shape = (None, *lead, step, rows, inputs)
                index = lambda i, j, a=at, s=stack, z=zeros: (s, *z, a + i, 0, 0)
            in_specs.append(pl.BlockSpec(shape, index))
    depth = sum(
        math.prod(x.shape[:-3] if st is None else x.shape[1:-3]) * x.shape[-2]
        for x, st, _ in blocks[0]
    )
    start = wanted[0]
    apart = wanted[1] - start if len(wanted) > 1 else 1
    if apart == 1:
        steps = 1
        out_spec = pl.BlockSpec(
            tuple(map(pl.Element, (step, 2, inputs, len(wanted) * inputs))),
            lambda i, j: (first + i * step, 0, 0, start * inputs),
        )
    else:
        steps = len(wanted)
        out_spec = pl.BlockSpec(
            (step, 2, inputs, inputs), lambda i, j: (first // step + i, 0, 0, start + apart * j)
        )
    aliases = {}
    if total is not None:
        aliases = {len(operands): 0}
        operands.append(total)
        in_specs.append(pl.BlockSpec(memory_space=pl.ANY))

    def body(*refs):
        refs = list(refs)
        if total is not None:
            refs.pop(-3)
        pairs_kernel(scale, count, step, wanted, *refs)

    return pl.pallas_call(
        body,
        grid=(size // step, steps),
        out_shape=jax.ShapeDtypeStruct((kept, 2, inputs, len(blocks) * inputs), jnp.float32),
        in_specs=in_specs,
        out_specs=out_spec,
        scratch_shapes=[pltpu.VMEM((step, 2, inputs, depth), jnp.bfloat16)],
        input_output_aliases=aliases,
        compiler_params=pltpu.CompilerParams(
            vmem_limit_bytes=32 * 1024 * 1024, dimension_semantics=("arbitrary", "arbitrary")
        ),
        cost_estimate=NO_COST,
    )(*operands)


def shifted(x, axis, by):
    devices = lax.axis_size(axis)
    return lax.ppermute(x, axis, [(i, (i + by) % devices) for i in range(devices)])


def swapped(x, axis, bit):
    devices = lax.axis_size(axis)
    return lax.ppermute(x, axis, [(i, i ^ bit) for i in range(devices)])


def after(x, *earlier):
    return lax.optimization_barrier((x, *earlier))[0]


def partners(own, axis):
    devices = lax.axis_size(axis)
    return [(own, None)] + [(shifted(own, axis, -hop), None) for hop in range(1, devices // 2 + 1)]


def tick(x, *earlier):
    x = lax.optimization_barrier((x, *earlier))[0]

    def body(x_ref, out_ref):
        out_ref[...] = x_ref[...] + 1.0

    return pl.pallas_call(
        body,
        out_shape=jax.ShapeDtypeStruct(x.shape, x.dtype),
        cost_estimate=pl.CostEstimate(
            flops=10**15, bytes_accessed=2 * x.size * 4, transcendentals=0
        ),
    )(x)


def after(x, *earlier):
    return lax.optimization_barrier((x, *earlier))[0]


class Exchange:
    def __init__(self, own, axis):
        self.own, self.axis = own, axis
        place = lax.axis_index(axis)
        self.is_far = (place & 2) == 2
        self.is_odd = (place & 1) == 1

    def y(self, *earlier):
        self.over_y = swapped(after(self.own, *earlier), self.axis, 4)

    def x(self, *earlier):
        own, over_y = lax.optimization_barrier((self.own, self.over_y, *earlier))[:2]
        self.over_x = swapped(jnp.where(self.is_far, own, over_y), self.axis, 2)

    def for_core(self, *earlier):
        own, over_x, over_y = lax.optimization_barrier(
            (self.own, self.over_x, self.over_y, *earlier)
        )[:3]
        return [jnp.where(self.is_odd, own, over_x), jnp.where(self.is_odd, over_x, over_y)]

    def core(self, *earlier):
        sent = jnp.stack(self.for_core(*earlier))
        self.over_core, self.slots = swapped(sent, self.axis, 1), (0, 1)

    over_x = over_core = None
    slots = (0, 1)

    def blocks(self):
        return [
            (self.own, None),
            (self.over_core, self.slots[0]),
            (self.over_x, None),
            (self.over_core, self.slots[1]),
            (self.over_y, None),
        ]


def core_of_both(a, b, *earlier):
    sent = jnp.stack(a.for_core(*earlier) + b.for_core(*earlier))
    a.over_core = b.over_core = swapped(sent, a.axis, 1)
    a.slots, b.slots = (0, 1), (2, 3)


def on_device(voltages, window):
    tap_count, channels = window.shape
    frames_dev = voltages.shape[2] // channels
    devices = lax.axis_size("tf")
    kept = channels // devices
    planned = devices == 4 and lax.axis_size("inp") == 8 and kept == 32
    sizes = [6, 6, 6, 6, 4, 4] if planned else [kept]
    nears = [12, 12, 8] if planned else [kept]
    count = len(sizes)
    firsts = [sum(sizes[:q]) for q in range(count)]
    near_firsts = [sum(nears[:h]) for h in range(len(nears))]
    cuts = [[(1, first, size)] for first, size in zip(near_firsts, nears)]
    for hop in range(2, devices):
        cuts += [[(hop, first, size)] for first, size in zip(firsts, sizes)]
    rest_cuts = [[(hop, 0, kept) for hop in range(1, devices)]]
    groups = frames_dev // GROUP // 2
    leading = voltages[:, :, : (tap_count - 1) * channels]
    halo = lax.ppermute(leading, "tf", [(i, i - 1) for i in range(1, devices)])
    table = jnp.asarray(dft_tables(channels))
    me = lax.axis_index("tf").astype(jnp.int32).reshape(1)
    own_a, rest = spectra_part(
        voltages, None, window, table, me, devices, 0, groups, rest_cuts, None
    )
    rest = rest.reshape(devices - 1, kept, *rest.shape[1:])
    own_b, *pieces = spectra_part(
        voltages, halo, window, table, me, devices, groups, groups, cuts, rest
    )
    near = pieces[: len(nears)]
    far = [pieces[len(nears) + q :: count] for q in range(count)]
    scale = 1.0 / math.sqrt(frames_dev * devices)

    def run_pairs(total, q, wanted, *groups_):
        blocks = [
            [(*entry, at) for entry, (_, at) in zip(entries, groups_)]
            for entries in zip(*[g for g, _ in groups_])
        ]
        return pairs(blocks, total, firsts[q], sizes[q], kept, scale, wanted)

    if not planned:
        near = swapped(near[0], "tf", 1)
        far = jnp.stack([swapped(x, "tf", hop + 2) for hop, x in enumerate(far[0])])
        wanted = tuple(range(lax.axis_size("inp") // 2 + 1))
        return run_pairs(
            None, 0, wanted, *[(partners(x, "inp"), 0) for x in (own_a, own_b, near, far)]
        )

    def over_z(q, *earlier):
        sent = lax.optimization_barrier((*far[q], *earlier))
        return [swapped(sent[hop - 2], "tf", hop) for hop in range(2, devices)]

    near_over_z = lambda h, *earlier: swapped(after(near[h], *earlier), "tf", 1)
    exchange = lambda *parts: Exchange(jnp.concatenate(parts), "inp")
    a, b = Exchange(own_a, "inp"), Exchange(own_b, "inp")
    t = jnp.zeros((8, 128), jnp.float32)

    def chunk(q, wanted):
        h = max(i for i, first in enumerate(near_firsts) if first <= firsts[q])
        at = nears[q] if q < len(nears) else 0
        return run_pairs(
            total,
            q,
            wanted,
            (a.blocks(), firsts[q]),
            (b.blocks(), firsts[q]),
            (lines[h].blocks(), firsts[q] - near_firsts[h]),
            (lines[q].blocks(), at),
            (lines[q].blocks(), at + sizes[q]),
        )

    total = None
    a.y()
    t = tick(t, own_b[:1, :8, :128])
    z, n, lines = [over_z(0, t)], [near_over_z(0, t)], []
    b.y(t)
    a.x(t)
    t = tick(t, *z[0])
    z.append(over_z(1, t))
    n.append(near_over_z(1, n[0], t))
    lines.append(exchange(n[0], *z[0]))
    lines[0].y(b.over_y, t)
    b.x(a.over_x, t)
    t = tick(t, *z[1], b.over_y, a.over_x)
    z.append(over_z(2, t))
    n.append(near_over_z(2, n[1], t))
    lines.append(exchange(n[1], *z[1]))
    lines[1].y(lines[0].over_y, t)
    lines[0].x(b.over_x, t)
    early, late, full = (0, 4), (1, 2, 3), (0, 1, 2, 3, 4)
    t = tick(t, *z[2], lines[0].over_y, b.over_x)
    z.append(over_z(3, t))
    lines.append(exchange(n[2], *z[2]))
    lines[2].y(lines[1].over_y, t)
    lines[1].x(lines[0].over_x, t)
    core_of_both(a, b, t)
    total = chunk(0, early)
    t = tick(t, *z[3], lines[1].over_y, lines[0].over_x, total)
    z.append(over_z(4, t))
    lines.append(exchange(*z[3]))
    lines[3].y(lines[2].over_y, t)
    lines[2].x(lines[1].over_x, t)
    lines[0].core(a.over_core, t)
    total = chunk(1, early)
    t = tick(t, *z[4], lines[2].over_y, lines[1].over_x, a.over_core, total)
    z.append(over_z(5, t))
    lines.append(exchange(*z[4]))
    lines[4].y(lines[3].over_y, t)
    lines[3].x(lines[2].over_x, t)
    total = chunk(2, early)
    total = chunk(0, late)
    lines[1].core(lines[0].over_core, t, total)
    t = tick(t, *z[5], lines[3].over_y, lines[2].over_x, lines[0].over_core)
    lines.append(exchange(*z[5]))
    lines[5].y(lines[4].over_y, t)
    lines[4].x(lines[3].over_x, t)
    lines[2].core(lines[1].over_core, t)
    total = chunk(1, late)
    t = tick(t, lines[4].over_y, lines[3].over_x, lines[1].over_core, total)
    lines[5].x(lines[4].over_x, t)
    lines[3].core(lines[2].over_core, t)
    total = chunk(2, late)
    t = tick(t, lines[5].over_y, lines[4].over_x, lines[2].over_core, total)
    core_of_both(lines[4], lines[5], t, lines[3].over_core)
    total = chunk(3, full)
    total = chunk(4, full)
    total = chunk(5, full)
    return total


def solution(mesh):
    in_specs = (P(None, "inp", "tf"), P())
    out_specs = P("tf", None, "inp", None)
    return jax.shard_map(
        on_device, mesh=mesh, in_specs=in_specs, out_specs=out_specs, check_vma=False
    )
```

```python
import functools
import math

import jax
import jax.numpy as jnp
import numpy as np
from jax import lax
from jax.experimental import pallas as pl
from jax.experimental.pallas import tpu as pltpu
from jax.sharding import PartitionSpec as P

GROUP = 4
PAD = 8


def dft_tables(length):
    indices = np.arange(length)
    phase = 2.0 * np.pi / length * (indices[:, None] * indices[None, :] % length)
    cosine = np.cos(phase) / math.sqrt(length)
    sine = np.sin(phase) / math.sqrt(length)
    upper = np.concatenate([cosine, sine], axis=1)
    lower = np.concatenate([-sine, cosine], axis=1)
    table = np.concatenate([upper, lower], axis=0).astype(np.float32)
    high = table.astype(jnp.bfloat16)
    low = (table - high.astype(np.float32)).astype(jnp.bfloat16)
    return np.stack([high, low])


def spectra_kernel(place, groups, kept, cuts, merge, *refs):
    refs = list(refs)
    me_ref = refs.pop(0)
    here, after = refs.pop(0), refs.pop(0)
    halo = refs.pop(0) if place["halo"] else None
    window, table = refs.pop(0), refs.pop(0)
    earlier = refs.pop(0) if merge else None
    store = refs.pop()
    own_ref = refs.pop(0)
    outs = refs
    step = pl.program_id(0)
    channels = window.shape[1]
    taps = window.shape[0]
    inputs = here.shape[1]
    frames = groups * GROUP
    rows = 2 * frames
    lane_tiles = inputs // 128

    def run(tail):
        weights = [window[t : t + 1, :] for t in range(taps)]
        filtered = []
        for part in range(2):
            loaded = [here[part, :, i * channels : (i + 1) * channels] for i in range(GROUP)]
            loaded += [tail[part, :, i * channels : (i + 1) * channels] for i in range(taps - 1)]
            loaded = [x.astype(jnp.float32) for x in loaded]
            filtered.append(
                [sum(weights[t] * loaded[i + t] for t in range(taps)) for i in range(GROUP)]
            )
        for i in range(GROUP):
            both = jnp.concatenate([filtered[0][i], filtered[1][i]], axis=1)
            high = both.astype(jnp.bfloat16)
            low = (both - high.astype(jnp.float32)).astype(jnp.bfloat16)
            nt = functools.partial(
                lax.dot_general,
                dimension_numbers=(((1,), (1,)), ((), ())),
                preferred_element_type=jnp.float32,
            )
            out = nt(table[0], high) + (nt(table[1], high) + nt(table[0], low))
            for part in range(2):
                first = part * frames + step * GROUP + i
                for lane in range(lane_tiles):
                    store[lane, pl.ds(first, channels, stride=rows + PAD), :] = out[
                        part * channels : (part + 1) * channels, lane * 128 : (lane + 1) * 128
                    ]

    if halo is None:
        run(after)
    else:
        last = pl.num_programs(0) - 1

        @pl.when(step < last)
        def _():
            run(after)

        @pl.when(step == last)
        def _():
            run(halo)

    @pl.when(step == pl.num_programs(0) - 1)
    def _():
        devices = channels // kept

        def piece(channel):
            start = pl.multiple_of(channel * (rows + PAD), 8)
            got = [store[lane, pl.ds(start, rows), :] for lane in range(lane_tiles)]
            return jnp.concatenate(got, axis=1).astype(jnp.bfloat16)

        me = me_ref[0]

        def own(i, carry):
            own_ref[i] = piece(me * kept + i)
            return carry

        lax.fori_loop(0, kept, own, 0, unroll=2)
        for number, cut in enumerate(cuts):
            at = 0
            for hop, first, size in cut:
                base = (me ^ hop) * kept + first

                def one(i, carry, out=outs[number], at=at, base=base, hop=hop, first=first):
                    if merge:
                        out[at + i, :rows, :] = earlier[hop - 1, first + i]
                        out[at + i, rows:, :] = piece(base + i)
                    else:
                        out[at + i] = piece(base + i)
                    return carry

                lax.fori_loop(0, size, one, 0, unroll=2)
                at += size


def spectra_part(voltages, halo, window, table, me, devices, first, groups, cuts, earlier):
    parts, inputs, samples = voltages.shape
    channels = window.shape[1]
    kept = channels // devices
    rows = 2 * groups * GROUP
    width = GROUP * channels
    last = samples // width - 1
    merge = earlier is not None
    operands = [me, voltages, voltages]
    in_specs = [
        pl.BlockSpec(memory_space=pltpu.SMEM),
        pl.BlockSpec((2, inputs, width), lambda i: (0, 0, first + i)),
        pl.BlockSpec((2, inputs, width), lambda i: (0, 0, jnp.minimum(first + i + 1, last))),
    ]
    whole = lambda shape: pl.BlockSpec(shape, lambda i: (0,) * len(shape))
    if halo is not None:
        operands.append(halo)
        in_specs.append(whole(halo.shape))
    operands += [window, table]
    in_specs += [whole(window.shape), whole(table.shape)]
    shapes = [(kept, rows, inputs)]
    if merge:
        operands.append(earlier)
        in_specs.append(whole(earlier.shape))
    depth = 2 * rows if merge else rows
    shapes += [(sum(size for _, _, size in cut), depth, inputs) for cut in cuts]
    return pl.pallas_call(
        functools.partial(
            spectra_kernel, {"halo": halo is not None}, groups, kept, cuts, merge
        ),
        grid=(groups,),
        out_shape=[jax.ShapeDtypeStruct(s, jnp.bfloat16) for s in shapes],
        in_specs=in_specs,
        out_specs=[whole(s) for s in shapes],
        scratch_shapes=[pltpu.VMEM((inputs // 128, channels * (rows + PAD), 128), jnp.float32)],
        compiler_params=pltpu.CompilerParams(
            vmem_limit_bytes=48 * 1024 * 1024, dimension_semantics=("arbitrary",)
        ),
        cost_estimate=pl.CostEstimate(
            flops=2 * 3 * 4 * channels * channels * inputs * groups * GROUP,
            bytes_accessed=2 * voltages.size,
            transcendentals=0,
        ),
    )(*operands)


def pairs_kernel(scale, count, step, wanted, *refs):
    out, lefts = refs[-2:]
    mine = refs[:count]
    per_block = [refs[n * count : (n + 1) * count] for n in range(1, len(refs) // count)]

    def pieces(block, channel):
        got = []
        for ref in block:
            if len(ref.shape) == 3:
                got.append(ref[channel])
            else:
                got += [ref[m, channel] for m in range(ref.shape[0])]
        return got

    @pl.when(pl.program_id(1) == 0)
    def _():
        for channel in range(step):
            values = pieces(mine, channel)
            turned = []
            for value in values:
                size = 2 * PART_FRAMES
                for first in range(0, value.shape[0], size):
                    turned.append(value[first + PART_FRAMES : first + size])
                    turned.append(-value[first : first + PART_FRAMES])
            lefts[channel, 0] = jnp.concatenate(values, axis=0).T
            lefts[channel, 1] = jnp.concatenate(turned, axis=0).T

    width = lefts.shape[2]
    together = out.shape[-1] // width
    for j in range(len(wanted) // together):

        @pl.when(pl.program_id(1) == j)
        def _(j=j):
            for channel in range(step):
                for k in range(together):
                    right = jnp.concatenate(pieces(per_block[j * together + k], channel), axis=0)
                    for part in range(2):
                        out[channel, part, :, k * width : (k + 1) * width] = (
                            jnp.dot(
                                lefts[channel, part], right, preferred_element_type=jnp.float32
                            )
                            * scale
                        )


PART_FRAMES = 16
NO_COST = pl.CostEstimate(flops=0, bytes_accessed=0, transcendentals=0)


def pairs(blocks, total, first, size, kept, scale, wanted):
    inputs = blocks[0][0][0].shape[-1]
    operands, in_specs = [], []
    count = len(blocks[0])
    used = [blocks[0]] + [blocks[n] for n in wanted]
    offsets = [offset for block in used for _, _, offset in block]
    step = 2 if all(x % 2 == 0 for x in [size, first, *offsets]) else 1
    for block in used:
        for array, stack, offset in block:
            operands.append(array)
            rows = array.shape[-2]
            at = offset // step
            lead = array.shape[:-3] if stack is None else array.shape[1:-3]
            zeros = (0,) * len(lead)
            if stack is None:
                shape = (*lead, step, rows, inputs)
                index = lambda i, j, a=at, z=zeros: (*z, a + i, 0, 0)
            else:
                shape = (None, *lead, step, rows, inputs)
                index = lambda i, j, a=at, s=stack, z=zeros: (s, *z, a + i, 0, 0)
            in_specs.append(pl.BlockSpec(shape, index))
    depth = sum(
        math.prod(x.shape[:-3] if st is None else x.shape[1:-3]) * x.shape[-2]
        for x, st, _ in blocks[0]
    )
    start = wanted[0]
    apart = wanted[1] - start if len(wanted) > 1 else 1
    if apart == 1:
        steps = 1
        out_spec = pl.BlockSpec(
            tuple(map(pl.Element, (step, 2, inputs, len(wanted) * inputs))),
            lambda i, j: (first + i * step, 0, 0, start * inputs),
        )
    else:
        steps = len(wanted)
        out_spec = pl.BlockSpec(
            (step, 2, inputs, inputs), lambda i, j: (first // step + i, 0, 0, start + apart * j)
        )
    aliases = {}
    if total is not None:
        aliases = {len(operands): 0}
        operands.append(total)
        in_specs.append(pl.BlockSpec(memory_space=pl.ANY))

    def body(*refs):
        refs = list(refs)
        if total is not None:
            refs.pop(-3)
        pairs_kernel(scale, count, step, wanted, *refs)

    return pl.pallas_call(
        body,
        grid=(size // step, steps),
        out_shape=jax.ShapeDtypeStruct((kept, 2, inputs, len(blocks) * inputs), jnp.float32),
        in_specs=in_specs,
        out_specs=out_spec,
        scratch_shapes=[pltpu.VMEM((step, 2, inputs, depth), jnp.bfloat16)],
        input_output_aliases=aliases,
        compiler_params=pltpu.CompilerParams(
            vmem_limit_bytes=32 * 1024 * 1024, dimension_semantics=("arbitrary", "arbitrary")
        ),
        cost_estimate=NO_COST,
    )(*operands)


def shifted(x, axis, by):
    devices = lax.axis_size(axis)
    return lax.ppermute(x, axis, [(i, (i + by) % devices) for i in range(devices)])


def swapped(x, axis, bit):
    devices = lax.axis_size(axis)
    return lax.ppermute(x, axis, [(i, i ^ bit) for i in range(devices)])


def after(x, *earlier):
    return lax.optimization_barrier((x, *earlier))[0]


def partners(own, axis):
    devices = lax.axis_size(axis)
    return [(own, None)] + [(shifted(own, axis, -hop), None) for hop in range(1, devices // 2 + 1)]


def tick(x, *earlier):
    x = lax.optimization_barrier((x, *earlier))[0]

    def body(x_ref, out_ref):
        out_ref[...] = x_ref[...] + 1.0

    return pl.pallas_call(
        body,
        out_shape=jax.ShapeDtypeStruct(x.shape, x.dtype),
        cost_estimate=pl.CostEstimate(
            flops=10**15, bytes_accessed=2 * x.size * 4, transcendentals=0
        ),
    )(x)


def after(x, *earlier):
    return lax.optimization_barrier((x, *earlier))[0]


class Exchange:
    def __init__(self, own, axis):
        self.own, self.axis = own, axis
        place = lax.axis_index(axis)
        self.is_far = (place & 2) == 2
        self.is_odd = (place & 1) == 1

    def y(self, *earlier):
        self.over_y = swapped(after(self.own, *earlier), self.axis, 4)

    def x(self, *earlier):
        own, over_y = lax.optimization_barrier((self.own, self.over_y, *earlier))[:2]
        self.over_x = swapped(jnp.where(self.is_far, own, over_y), self.axis, 2)

    def for_core(self, *earlier):
        own, over_x, over_y = lax.optimization_barrier(
            (self.own, self.over_x, self.over_y, *earlier)
        )[:3]
        return [jnp.where(self.is_odd, own, over_x), jnp.where(self.is_odd, over_x, over_y)]

    def core(self, *earlier):
        sent = jnp.stack(self.for_core(*earlier))
        self.over_core, self.slots = swapped(sent, self.axis, 1), (0, 1)

    over_x = over_core = None
    slots = (0, 1)

    def blocks(self):
        return [
            (self.own, None),
            (self.over_core, self.slots[0]),
            (self.over_x, None),
            (self.over_core, self.slots[1]),
            (self.over_y, None),
        ]


def core_of_both(a, b, *earlier):
    sent = jnp.stack(a.for_core(*earlier) + b.for_core(*earlier))
    a.over_core = b.over_core = swapped(sent, a.axis, 1)
    a.slots, b.slots = (0, 1), (2, 3)


def on_device(voltages, window):
    tap_count, channels = window.shape
    frames_dev = voltages.shape[2] // channels
    devices = lax.axis_size("tf")
    kept = channels // devices
    planned = devices == 4 and lax.axis_size("inp") == 8 and kept == 32
    sizes = [6, 6, 6, 6, 4, 4] if planned else [kept]
    nears = [12, 12, 8] if planned else [kept]
    count = len(sizes)
    firsts = [sum(sizes[:q]) for q in range(count)]
    near_firsts = [sum(nears[:h]) for h in range(len(nears))]
    cuts = [[(1, first, size)] for first, size in zip(near_firsts, nears)]
    for hop in range(2, devices):
        cuts += [[(hop, first, size)] for first, size in zip(firsts, sizes)]
    rest_cuts = [[(hop, 0, kept) for hop in range(1, devices)]]
    groups = frames_dev // GROUP // 2
    leading = voltages[:, :, : (tap_count - 1) * channels]
    halo = lax.ppermute(leading, "tf", [(i, i - 1) for i in range(1, devices)])
    table = jnp.asarray(dft_tables(channels))
    me = lax.axis_index("tf").astype(jnp.int32).reshape(1)
    own_a, rest = spectra_part(
        voltages, None, window, table, me, devices, 0, groups, rest_cuts, None
    )
    rest = rest.reshape(devices - 1, kept, *rest.shape[1:])
    own_b, *pieces = spectra_part(
        voltages, halo, window, table, me, devices, groups, groups, cuts, rest
    )
    near = pieces[: len(nears)]
    far = [pieces[len(nears) + q :: count] for q in range(count)]
    scale = 1.0 / math.sqrt(frames_dev * devices)

    def run_pairs(total, q, wanted, *groups_):
        blocks = [
            [(*entry, at) for entry, (_, at) in zip(entries, groups_)]
            for entries in zip(*[g for g, _ in groups_])
        ]
        return pairs(blocks, total, firsts[q], sizes[q], kept, scale, wanted)

    if not planned:
        near = swapped(near[0], "tf", 1)
        far = jnp.stack([swapped(x, "tf", hop + 2) for hop, x in enumerate(far[0])])
        wanted = tuple(range(lax.axis_size("inp") // 2 + 1))
        return run_pairs(
            None, 0, wanted, *[(partners(x, "inp"), 0) for x in (own_a, own_b, near, far)]
        )

    def over_z(q, *earlier):
        sent = lax.optimization_barrier((*far[q], *earlier))
        return [swapped(sent[hop - 2], "tf", hop) for hop in range(2, devices)]

    near_over_z = lambda h, *earlier: swapped(after(near[h], *earlier), "tf", 1)
    exchange = lambda *parts: Exchange(jnp.concatenate(parts), "inp")
    a, b = Exchange(own_a, "inp"), Exchange(own_b, "inp")
    t = jnp.zeros((8, 128), jnp.float32)

    def chunk(q, wanted):
        h = max(i for i, first in enumerate(near_firsts) if first <= firsts[q])
        at = nears[q] if q < len(nears) else 0
        return run_pairs(
            total,
            q,
            wanted,
            (a.blocks(), firsts[q]),
            (b.blocks(), firsts[q]),
            (lines[h].blocks(), firsts[q] - near_firsts[h]),
            (lines[q].blocks(), at),
            (lines[q].blocks(), at + sizes[q]),
        )

    total = None
    a.y()
    t = tick(t, own_b[:1, :8, :128])
    z, n, lines = [over_z(0, t)], [near_over_z(0, t)], []
    b.y(t)
    a.x(t)
    t = tick(t, *z[0])
    z.append(over_z(1, t))
    n.append(near_over_z(1, n[0], t))
    lines.append(exchange(n[0], *z[0]))
    lines[0].y(b.over_y, t)
    b.x(a.over_x, t)
    t = tick(t, *z[1], b.over_y, a.over_x)
    z.append(over_z(2, t))
    n.append(near_over_z(2, n[1], t))
    lines.append(exchange(n[1], *z[1]))
    lines[1].y(lines[0].over_y, t)
    lines[0].x(b.over_x, t)
    early, late, full = (0, 4), (1, 2, 3), (0, 1, 2, 3, 4)
    t = tick(t, *z[2], lines[0].over_y, b.over_x)
    z.append(over_z(3, t))
    lines.append(exchange(n[2], *z[2]))
    lines[2].y(lines[1].over_y, t)
    lines[1].x(lines[0].over_x, t)
    core_of_both(a, b, t)
    total = chunk(0, early)
    t = tick(t, *z[3], lines[1].over_y, lines[0].over_x, total)
    z.append(over_z(4, t))
    lines.append(exchange(*z[3]))
    lines[3].y(lines[2].over_y, t)
    lines[2].x(lines[1].over_x, t)
    lines[0].core(a.over_core, t)
    total = chunk(1, early)
    t = tick(t, *z[4], lines[2].over_y, lines[1].over_x, a.over_core, total)
    z.append(over_z(5, t))
    lines.append(exchange(*z[4]))
    total = chunk(2, early)
    lines[4].y(lines[3].over_y, t, total)
    lines[3].x(lines[2].over_x, t)
    total = chunk(0, late)
    lines[1].core(lines[0].over_core, t, total)
    t = tick(t, *z[5], lines[3].over_y, lines[2].over_x, lines[0].over_core)
    lines.append(exchange(*z[5]))
    lines[5].y(lines[4].over_y, t)
    lines[4].x(lines[3].over_x, t)
    lines[2].core(lines[1].over_core, t)
    total = chunk(1, late)
    t = tick(t, lines[4].over_y, lines[3].over_x, lines[1].over_core, total)
    lines[5].x(lines[4].over_x, t)
    lines[3].core(lines[2].over_core, t)
    total = chunk(2, late)
    t = tick(t, lines[5].over_y, lines[4].over_x, lines[2].over_core, total)
    core_of_both(lines[4], lines[5], t, lines[3].over_core)
    total = chunk(3, full)
    total = chunk(4, full)
    total = chunk(5, full)
    return total


def solution(mesh):
    in_specs = (P(None, "inp", "tf"), P())
    out_specs = P("tf", None, "inp", None)
    return jax.shard_map(
        on_device, mesh=mesh, in_specs=in_specs, out_specs=out_specs, check_vma=False
    )
```

```python
import functools
import math

import jax
import jax.numpy as jnp
import numpy as np
from jax import lax
from jax.experimental import pallas as pl
from jax.experimental.pallas import tpu as pltpu
from jax.sharding import PartitionSpec as P

GROUP = 4
PAD = 8


def dft_tables(length):
    indices = np.arange(length)
    phase = 2.0 * np.pi / length * (indices[:, None] * indices[None, :] % length)
    cosine = np.cos(phase) / math.sqrt(length)
    sine = np.sin(phase) / math.sqrt(length)
    upper = np.concatenate([cosine, sine], axis=1)
    lower = np.concatenate([-sine, cosine], axis=1)
    table = np.concatenate([upper, lower], axis=0).astype(np.float32)
    high = table.astype(jnp.bfloat16)
    low = (table - high.astype(np.float32)).astype(jnp.bfloat16)
    return np.stack([high, low])


def spectra_kernel(place, groups, kept, cuts, merge, *refs):
    refs = list(refs)
    me_ref = refs.pop(0)
    here, after = refs.pop(0), refs.pop(0)
    halo = refs.pop(0) if place["halo"] else None
    window, table = refs.pop(0), refs.pop(0)
    earlier = refs.pop(0) if merge else None
    store = refs.pop()
    own_ref = refs.pop(0)
    outs = refs
    step = pl.program_id(0)
    channels = window.shape[1]
    taps = window.shape[0]
    inputs = here.shape[1]
    frames = groups * GROUP
    rows = 2 * frames
    lane_tiles = inputs // 128

    def run(tail):
        weights = [window[t : t + 1, :] for t in range(taps)]
        filtered = []
        for part in range(2):
            loaded = [here[part, :, i * channels : (i + 1) * channels] for i in range(GROUP)]
            loaded += [tail[part, :, i * channels : (i + 1) * channels] for i in range(taps - 1)]
            loaded = [x.astype(jnp.float32) for x in loaded]
            filtered.append(
                [sum(weights[t] * loaded[i + t] for t in range(taps)) for i in range(GROUP)]
            )
        for i in range(GROUP):
            both = jnp.concatenate([filtered[0][i], filtered[1][i]], axis=1)
            high = both.astype(jnp.bfloat16)
            low = (both - high.astype(jnp.float32)).astype(jnp.bfloat16)
            nt = functools.partial(
                lax.dot_general,
                dimension_numbers=(((1,), (1,)), ((), ())),
                preferred_element_type=jnp.float32,
            )
            out = nt(table[0], high) + (nt(table[1], high) + nt(table[0], low))
            for part in range(2):
                first = part * frames + step * GROUP + i
                for lane in range(lane_tiles):
                    store[lane, pl.ds(first, channels, stride=rows + PAD), :] = out[
                        part * channels : (part + 1) * channels, lane * 128 : (lane + 1) * 128
                    ]

    if halo is None:
        run(after)
    else:
        last = pl.num_programs(0) - 1

        @pl.when(step < last)
        def _():
            run(after)

        @pl.when(step == last)
        def _():
            run(halo)

    @pl.when(step == pl.num_programs(0) - 1)
    def _():
        devices = channels // kept

        def piece(channel):
            start = pl.multiple_of(channel * (rows + PAD), 8)
            got = [store[lane, pl.ds(start, rows), :] for lane in range(lane_tiles)]
            return jnp.concatenate(got, axis=1).astype(jnp.bfloat16)

        me = me_ref[0]

        def own(i, carry):
            own_ref[i] = piece(me * kept + i)
            return carry

        lax.fori_loop(0, kept, own, 0, unroll=2)
        for number, cut in enumerate(cuts):
            at = 0
            for hop, first, size in cut:
                base = (me ^ hop) * kept + first

                def one(i, carry, out=outs[number], at=at, base=base, hop=hop, first=first):
                    if merge:
                        out[at + i, :rows, :] = earlier[hop - 1, first + i]
                        out[at + i, rows:, :] = piece(base + i)
                    else:
                        out[at + i] = piece(base + i)
                    return carry

                lax.fori_loop(0, size, one, 0, unroll=2)
                at += size


def spectra_part(voltages, halo, window, table, me, devices, first, groups, cuts, earlier):
    parts, inputs, samples = voltages.shape
    channels = window.shape[1]
    kept = channels // devices
    rows = 2 * groups * GROUP
    width = GROUP * channels
    last = samples // width - 1
    merge = earlier is not None
    operands = [me, voltages, voltages]
    in_specs = [
        pl.BlockSpec(memory_space=pltpu.SMEM),
        pl.BlockSpec((2, inputs, width), lambda i: (0, 0, first + i)),
        pl.BlockSpec((2, inputs, width), lambda i: (0, 0, jnp.minimum(first + i + 1, last))),
    ]
    whole = lambda shape: pl.BlockSpec(shape, lambda i: (0,) * len(shape))
    if halo is not None:
        operands.append(halo)
        in_specs.append(whole(halo.shape))
    operands += [window, table]
    in_specs += [whole(window.shape), whole(table.shape)]
    shapes = [(kept, rows, inputs)]
    if merge:
        operands.append(earlier)
        in_specs.append(whole(earlier.shape))
    depth = 2 * rows if merge else rows
    shapes += [(sum(size for _, _, size in cut), depth, inputs) for cut in cuts]
    return pl.pallas_call(
        functools.partial(
            spectra_kernel, {"halo": halo is not None}, groups, kept, cuts, merge
        ),
        grid=(groups,),
        out_shape=[jax.ShapeDtypeStruct(s, jnp.bfloat16) for s in shapes],
        in_specs=in_specs,
        out_specs=[whole(s) for s in shapes],
        scratch_shapes=[pltpu.VMEM((inputs // 128, channels * (rows + PAD), 128), jnp.float32)],
        compiler_params=pltpu.CompilerParams(
            vmem_limit_bytes=48 * 1024 * 1024, dimension_semantics=("arbitrary",)
        ),
        cost_estimate=pl.CostEstimate(
            flops=2 * 3 * 4 * channels * channels * inputs * groups * GROUP,
            bytes_accessed=2 * voltages.size,
            transcendentals=0,
        ),
    )(*operands)


def pairs_kernel(scale, count, step, wanted, *refs):
    out, lefts = refs[-2:]
    mine = refs[:count]
    per_block = [refs[n * count : (n + 1) * count] for n in range(1, len(refs) // count)]

    def pieces(block, channel):
        got = []
        for ref in block:
            if len(ref.shape) == 3:
                got.append(ref[channel])
            else:
                got += [ref[m, channel] for m in range(ref.shape[0])]
        return got

    @pl.when(pl.program_id(1) == 0)
    def _():
        for channel in range(step):
            values = pieces(mine, channel)
            turned = []
            for value in values:
                size = 2 * PART_FRAMES
                for first in range(0, value.shape[0], size):
                    turned.append(value[first + PART_FRAMES : first + size])
                    turned.append(-value[first : first + PART_FRAMES])
            lefts[channel, 0] = jnp.concatenate(values, axis=0).T
            lefts[channel, 1] = jnp.concatenate(turned, axis=0).T

    width = lefts.shape[2]
    together = out.shape[-1] // width
    for j in range(len(wanted) // together):

        @pl.when(pl.program_id(1) == j)
        def _(j=j):
            for channel in range(step):
                for k in range(together):
                    right = jnp.concatenate(pieces(per_block[j * together + k], channel), axis=0)
                    for part in range(2):
                        out[channel, part, :, k * width : (k + 1) * width] = (
                            jnp.dot(
                                lefts[channel, part], right, preferred_element_type=jnp.float32
                            )
                            * scale
                        )


PART_FRAMES = 16
NO_COST = pl.CostEstimate(flops=0, bytes_accessed=0, transcendentals=0)


def pairs(blocks, total, first, size, kept, scale, wanted):
    inputs = blocks[0][0][0].shape[-1]
    operands, in_specs = [], []
    count = len(blocks[0])
    used = [blocks[0]] + [blocks[n] for n in wanted]
    offsets = [offset for block in used for _, _, offset in block]
    step = 2 if all(x % 2 == 0 for x in [size, first, *offsets]) else 1
    for block in used:
        for array, stack, offset in block:
            operands.append(array)
            rows = array.shape[-2]
            at = offset // step
            lead = array.shape[:-3] if stack is None else array.shape[1:-3]
            zeros = (0,) * len(lead)
            if stack is None:
                shape = (*lead, step, rows, inputs)
                index = lambda i, j, a=at, z=zeros: (*z, a + i, 0, 0)
            else:
                shape = (None, *lead, step, rows, inputs)
                index = lambda i, j, a=at, s=stack, z=zeros: (s, *z, a + i, 0, 0)
            in_specs.append(pl.BlockSpec(shape, index))
    depth = sum(
        math.prod(x.shape[:-3] if st is None else x.shape[1:-3]) * x.shape[-2]
        for x, st, _ in blocks[0]
    )
    start = wanted[0]
    apart = wanted[1] - start if len(wanted) > 1 else 1
    if apart == 1:
        steps = 1
        out_spec = pl.BlockSpec(
            tuple(map(pl.Element, (step, 2, inputs, len(wanted) * inputs))),
            lambda i, j: (first + i * step, 0, 0, start * inputs),
        )
    else:
        steps = len(wanted)
        out_spec = pl.BlockSpec(
            (step, 2, inputs, inputs), lambda i, j: (first // step + i, 0, 0, start + apart * j)
        )
    aliases = {}
    if total is not None:
        aliases = {len(operands): 0}
        operands.append(total)
        in_specs.append(pl.BlockSpec(memory_space=pl.ANY))

    def body(*refs):
        refs = list(refs)
        if total is not None:
            refs.pop(-3)
        pairs_kernel(scale, count, step, wanted, *refs)

    return pl.pallas_call(
        body,
        grid=(size // step, steps),
        out_shape=jax.ShapeDtypeStruct((kept, 2, inputs, len(blocks) * inputs), jnp.float32),
        in_specs=in_specs,
        out_specs=out_spec,
        scratch_shapes=[pltpu.VMEM((step, 2, inputs, depth), jnp.bfloat16)],
        input_output_aliases=aliases,
        compiler_params=pltpu.CompilerParams(
            vmem_limit_bytes=32 * 1024 * 1024, dimension_semantics=("arbitrary", "arbitrary")
        ),
        cost_estimate=NO_COST,
    )(*operands)


def shifted(x, axis, by):
    devices = lax.axis_size(axis)
    return lax.ppermute(x, axis, [(i, (i + by) % devices) for i in range(devices)])


def swapped(x, axis, bit):
    devices = lax.axis_size(axis)
    return lax.ppermute(x, axis, [(i, i ^ bit) for i in range(devices)])


def after(x, *earlier):
    return lax.optimization_barrier((x, *earlier))[0]


def partners(own, axis):
    devices = lax.axis_size(axis)
    return [(own, None)] + [(shifted(own, axis, -hop), None) for hop in range(1, devices // 2 + 1)]


def tick(x, *earlier):
    x = lax.optimization_barrier((x, *earlier))[0]

    def body(x_ref, out_ref):
        out_ref[...] = x_ref[...] + 1.0

    return pl.pallas_call(
        body,
        out_shape=jax.ShapeDtypeStruct(x.shape, x.dtype),
        cost_estimate=pl.CostEstimate(
            flops=10**15, bytes_accessed=2 * x.size * 4, transcendentals=0
        ),
    )(x)


def after(x, *earlier):
    return lax.optimization_barrier((x, *earlier))[0]


class Exchange:
    def __init__(self, own, axis):
        self.own, self.axis = own, axis
        place = lax.axis_index(axis)
        self.is_far = (place & 2) == 2
        self.is_odd = (place & 1) == 1

    def y(self, *earlier):
        self.over_y = swapped(after(self.own, *earlier), self.axis, 4)

    def x(self, *earlier):
        own, over_y = lax.optimization_barrier((self.own, self.over_y, *earlier))[:2]
        self.over_x = swapped(jnp.where(self.is_far, own, over_y), self.axis, 2)

    def for_core(self, *earlier):
        own, over_x, over_y = lax.optimization_barrier(
            (self.own, self.over_x, self.over_y, *earlier)
        )[:3]
        return [jnp.where(self.is_odd, own, over_x), jnp.where(self.is_odd, over_x, over_y)]

    def core(self, *earlier):
        sent = jnp.stack(self.for_core(*earlier))
        self.over_core, self.slots = swapped(sent, self.axis, 1), (0, 1)

    over_x = over_core = None
    slots = (0, 1)

    def blocks(self):
        return [
            (self.own, None),
            (self.over_core, self.slots[0]),
            (self.over_x, None),
            (self.over_core, self.slots[1]),
            (self.over_y, None),
        ]


def core_of_both(a, b, *earlier):
    sent = jnp.stack(a.for_core(*earlier) + b.for_core(*earlier))
    a.over_core = b.over_core = swapped(sent, a.axis, 1)
    a.slots, b.slots = (0, 1), (2, 3)


def on_device(voltages, window):
    tap_count, channels = window.shape
    frames_dev = voltages.shape[2] // channels
    devices = lax.axis_size("tf")
    kept = channels // devices
    planned = devices == 4 and lax.axis_size("inp") == 8 and kept == 32
    sizes = [6, 6, 6, 6, 4, 4] if planned else [kept]
    nears = [12, 12, 8] if planned else [kept]
    count = len(sizes)
    firsts = [sum(sizes[:q]) for q in range(count)]
    near_firsts = [sum(nears[:h]) for h in range(len(nears))]
    cuts = [[(1, first, size)] for first, size in zip(near_firsts, nears)]
    for hop in range(2, devices):
        cuts += [[(hop, first, size)] for first, size in zip(firsts, sizes)]
    rest_cuts = [[(hop, 0, kept) for hop in range(1, devices)]]
    groups = frames_dev // GROUP // 2
    leading = voltages[:, :, : (tap_count - 1) * channels]
    halo = lax.ppermute(leading, "tf", [(i, i - 1) for i in range(1, devices)])
    table = pltpu.with_memory_space_constraint(jnp.asarray(dft_tables(channels)), pltpu.HBM)
    window = pltpu.with_memory_space_constraint(window, pltpu.HBM)
    me = lax.axis_index("tf").astype(jnp.int32).reshape(1)
    own_a, rest = spectra_part(
        voltages, None, window, table, me, devices, 0, groups, rest_cuts, None
    )
    rest = rest.reshape(devices - 1, kept, *rest.shape[1:])
    own_b, *pieces = spectra_part(
        voltages, halo, window, table, me, devices, groups, groups, cuts, rest
    )
    near = pieces[: len(nears)]
    far = [pieces[len(nears) + q :: count] for q in range(count)]
    scale = 1.0 / math.sqrt(frames_dev * devices)

    def run_pairs(total, q, wanted, *groups_):
        blocks = [
            [(*entry, at) for entry, (_, at) in zip(entries, groups_)]
            for entries in zip(*[g for g, _ in groups_])
        ]
        return pairs(blocks, total, firsts[q], sizes[q], kept, scale, wanted)

    if not planned:
        near = swapped(near[0], "tf", 1)
        far = jnp.stack([swapped(x, "tf", hop + 2) for hop, x in enumerate(far[0])])
        wanted = tuple(range(lax.axis_size("inp") // 2 + 1))
        return run_pairs(
            None, 0, wanted, *[(partners(x, "inp"), 0) for x in (own_a, own_b, near, far)]
        )

    def over_z(q, *earlier):
        sent = lax.optimization_barrier((*far[q], *earlier))
        return [swapped(sent[hop - 2], "tf", hop) for hop in range(2, devices)]

    near_over_z = lambda h, *earlier: swapped(after(near[h], *earlier), "tf", 1)
    exchange = lambda *parts: Exchange(jnp.concatenate(parts), "inp")
    a, b = Exchange(own_a, "inp"), Exchange(own_b, "inp")
    t = jnp.zeros((8, 128), jnp.float32)

    def chunk(q, wanted):
        h = max(i for i, first in enumerate(near_firsts) if first <= firsts[q])
        at = nears[q] if q < len(nears) else 0
        return run_pairs(
            total,
            q,
            wanted,
            (a.blocks(), firsts[q]),
            (b.blocks(), firsts[q]),
            (lines[h].blocks(), firsts[q] - near_firsts[h]),
            (lines[q].blocks(), at),
            (lines[q].blocks(), at + sizes[q]),
        )

    total = None
    a.y()
    t = tick(t, own_b[:1, :8, :128])
    z, n, lines = [over_z(0, t)], [near_over_z(0, t)], []
    b.y(t)
    a.x(t)
    t = tick(t, *z[0])
    z.append(over_z(1, t))
    n.append(near_over_z(1, n[0], t))
    lines.append(exchange(n[0], *z[0]))
    lines[0].y(b.over_y, t)
    b.x(a.over_x, t)
    t = tick(t, *z[1], b.over_y, a.over_x)
    z.append(over_z(2, t))
    n.append(near_over_z(2, n[1], t))
    lines.append(exchange(n[1], *z[1]))
    lines[1].y(lines[0].over_y, t)
    lines[0].x(b.over_x, t)
    early, late, full = (0, 4), (1, 2, 3), (0, 1, 2, 3, 4)
    t = tick(t, *z[2], lines[0].over_y, b.over_x)
    z.append(over_z(3, t))
    lines.append(exchange(n[2], *z[2]))
    lines[2].y(lines[1].over_y, t)
    lines[1].x(lines[0].over_x, t)
    core_of_both(a, b, t)
    total = chunk(0, early)
    t = tick(t, *z[3], lines[1].over_y, lines[0].over_x, total)
    z.append(over_z(4, t))
    lines.append(exchange(*z[3]))
    lines[3].y(lines[2].over_y, t)
    lines[2].x(lines[1].over_x, t)
    lines[0].core(a.over_core, t)
    total = chunk(1, early)
    t = tick(t, *z[4], lines[2].over_y, lines[1].over_x, a.over_core, total)
    z.append(over_z(5, t))
    lines.append(exchange(*z[4]))
    total = chunk(2, early)
    lines[4].y(lines[3].over_y, t, total)
    lines[3].x(lines[2].over_x, t)
    total = chunk(0, late)
    lines[1].core(lines[0].over_core, t, total)
    t = tick(t, *z[5], lines[3].over_y, lines[2].over_x, lines[0].over_core)
    lines.append(exchange(*z[5]))
    lines[5].y(lines[4].over_y, t)
    lines[4].x(lines[3].over_x, t)
    lines[2].core(lines[1].over_core, t)
    total = chunk(1, late)
    t = tick(t, lines[4].over_y, lines[3].over_x, lines[1].over_core, total)
    lines[5].x(lines[4].over_x, t)
    lines[3].core(lines[2].over_core, t)
    total = chunk(2, late)
    t = tick(t, lines[5].over_y, lines[4].over_x, lines[2].over_core, total)
    core_of_both(lines[4], lines[5], t, lines[3].over_core)
    total = chunk(3, full)
    total = chunk(4, full)
    total = chunk(5, full)
    return total


def solution(mesh):
    in_specs = (P(None, "inp", "tf"), P())
    out_specs = P("tf", None, "inp", None)
    return jax.shard_map(
        on_device, mesh=mesh, in_specs=in_specs, out_specs=out_specs, check_vma=False
    )
```

```python
import functools
import math

import jax
import jax.numpy as jnp
import numpy as np
from jax import lax
from jax.experimental import pallas as pl
from jax.experimental.pallas import tpu as pltpu
from jax.sharding import PartitionSpec as P

GROUP = 4
PAD = 8


def dft_tables(length):
    indices = np.arange(length)
    phase = 2.0 * np.pi / length * (indices[:, None] * indices[None, :] % length)
    cosine = np.cos(phase) / math.sqrt(length)
    sine = np.sin(phase) / math.sqrt(length)
    upper = np.concatenate([cosine, sine], axis=1)
    lower = np.concatenate([-sine, cosine], axis=1)
    table = np.concatenate([upper, lower], axis=0).astype(np.float32)
    high = table.astype(jnp.bfloat16)
    low = (table - high.astype(np.float32)).astype(jnp.bfloat16)
    return np.stack([high, low])


def spectra_kernel(place, groups, kept, cuts, merge, *refs):
    refs = list(refs)
    me_ref = refs.pop(0)
    here, after = refs.pop(0), refs.pop(0)
    halo = refs.pop(0) if place["halo"] else None
    window, table = refs.pop(0), refs.pop(0)
    earlier = refs.pop(0) if merge else None
    store = refs.pop()
    own_ref = refs.pop(0)
    outs = refs
    step = pl.program_id(0)
    channels = window.shape[1]
    taps = window.shape[0]
    inputs = here.shape[1]
    frames = groups * GROUP
    rows = 2 * frames
    lane_tiles = inputs // 128

    def run(tail):
        weights = [window[t : t + 1, :] for t in range(taps)]
        filtered = []
        for part in range(2):
            loaded = [here[part, :, i * channels : (i + 1) * channels] for i in range(GROUP)]
            loaded += [tail[part, :, i * channels : (i + 1) * channels] for i in range(taps - 1)]
            loaded = [x.astype(jnp.float32) for x in loaded]
            filtered.append(
                [sum(weights[t] * loaded[i + t] for t in range(taps)) for i in range(GROUP)]
            )
        for i in range(GROUP):
            both = jnp.concatenate([filtered[0][i], filtered[1][i]], axis=1)
            high = both.astype(jnp.bfloat16)
            low = (both - high.astype(jnp.float32)).astype(jnp.bfloat16)
            nt = functools.partial(
                lax.dot_general,
                dimension_numbers=(((1,), (1,)), ((), ())),
                preferred_element_type=jnp.float32,
            )
            out = nt(table[0], high) + (nt(table[1], high) + nt(table[0], low))
            for part in range(2):
                first = part * frames + step * GROUP + i
                for lane in range(lane_tiles):
                    store[lane, pl.ds(first, channels, stride=rows + PAD), :] = out[
                        part * channels : (part + 1) * channels, lane * 128 : (lane + 1) * 128
                    ]

    if halo is None:
        run(after)
    else:
        last = pl.num_programs(0) - 1

        @pl.when(step < last)
        def _():
            run(after)

        @pl.when(step == last)
        def _():
            run(halo)

    @pl.when(step == pl.num_programs(0) - 1)
    def _():
        devices = channels // kept

        def piece(channel):
            start = pl.multiple_of(channel * (rows + PAD), 8)
            got = [store[lane, pl.ds(start, rows), :] for lane in range(lane_tiles)]
            return jnp.concatenate(got, axis=1).astype(jnp.bfloat16)

        me = me_ref[0]

        def own(i, carry):
            own_ref[i] = piece(me * kept + i)
            return carry

        lax.fori_loop(0, kept, own, 0, unroll=2)
        for number, cut in enumerate(cuts):
            at = 0
            for hop, first, size in cut:
                base = (me ^ hop) * kept + first

                def one(i, carry, out=outs[number], at=at, base=base, hop=hop, first=first):
                    if merge:
                        out[at + i, :rows, :] = earlier[hop - 1, first + i]
                        out[at + i, rows:, :] = piece(base + i)
                    else:
                        out[at + i] = piece(base + i)
                    return carry

                lax.fori_loop(0, size, one, 0, unroll=2)
                at += size


def spectra_part(voltages, halo, window, table, me, devices, first, groups, cuts, earlier):
    parts, inputs, samples = voltages.shape
    channels = window.shape[1]
    kept = channels // devices
    rows = 2 * groups * GROUP
    width = GROUP * channels
    last = samples // width - 1
    merge = earlier is not None
    operands = [me, voltages, voltages]
    in_specs = [
        pl.BlockSpec(memory_space=pltpu.SMEM),
        pl.BlockSpec((2, inputs, width), lambda i: (0, 0, first + i)),
        pl.BlockSpec((2, inputs, width), lambda i: (0, 0, jnp.minimum(first + i + 1, last))),
    ]
    whole = lambda shape: pl.BlockSpec(shape, lambda i: (0,) * len(shape))
    if halo is not None:
        operands.append(halo)
        in_specs.append(whole(halo.shape))
    operands += [window, table]
    in_specs += [whole(window.shape), whole(table.shape)]
    shapes = [(kept, rows, inputs)]
    if merge:
        operands.append(earlier)
        in_specs.append(whole(earlier.shape))
    depth = 2 * rows if merge else rows
    shapes += [(sum(size for _, _, size in cut), depth, inputs) for cut in cuts]
    return pl.pallas_call(
        functools.partial(
            spectra_kernel, {"halo": halo is not None}, groups, kept, cuts, merge
        ),
        grid=(groups,),
        out_shape=[jax.ShapeDtypeStruct(s, jnp.bfloat16) for s in shapes],
        in_specs=in_specs,
        out_specs=[whole(s) for s in shapes],
        scratch_shapes=[pltpu.VMEM((inputs // 128, channels * (rows + PAD), 128), jnp.float32)],
        compiler_params=pltpu.CompilerParams(
            vmem_limit_bytes=48 * 1024 * 1024, dimension_semantics=("arbitrary",)
        ),
        cost_estimate=pl.CostEstimate(
            flops=2 * 3 * 4 * channels * channels * inputs * groups * GROUP,
            bytes_accessed=2 * voltages.size,
            transcendentals=0,
        ),
    )(*operands)


def pairs_kernel(scale, count, step, wanted, *refs):
    out, lefts = refs[-2:]
    mine = refs[:count]
    per_block = [refs[n * count : (n + 1) * count] for n in range(1, len(refs) // count)]

    def pieces(block, channel):
        got = []
        for ref in block:
            if len(ref.shape) == 3:
                got.append(ref[channel])
            else:
                got += [ref[m, channel] for m in range(ref.shape[0])]
        return got

    def rows_of(channel):
        values = pieces(mine, channel)
        turned = []
        for value in values:
            size = 2 * PART_FRAMES
            for first in range(0, value.shape[0], size):
                turned.append(value[first + PART_FRAMES : first + size])
                turned.append(-value[first : first + PART_FRAMES])
        return jnp.concatenate(values, axis=0).T, jnp.concatenate(turned, axis=0).T

    width = lefts.shape[2]
    together = out.shape[-1] // width

    def products(channel, j, left):
        for k in range(together):
            right = jnp.concatenate(pieces(per_block[j * together + k], channel), axis=0)
            for part in range(2):
                out[channel, part, :, k * width : (k + 1) * width] = (
                    jnp.dot(left[part], right, preferred_element_type=jnp.float32) * scale
                )

    if together == len(wanted):
        for channel in range(step):
            products(channel, 0, rows_of(channel))
        return

    @pl.when(pl.program_id(1) == 0)
    def _():
        for channel in range(step):
            lefts[channel, 0], lefts[channel, 1] = rows_of(channel)

    for j in range(len(wanted) // together):

        @pl.when(pl.program_id(1) == j)
        def _(j=j):
            for channel in range(step):
                products(channel, j, (lefts[channel, 0], lefts[channel, 1]))


PART_FRAMES = 16
NO_COST = pl.CostEstimate(flops=0, bytes_accessed=0, transcendentals=0)


def pairs(blocks, total, first, size, kept, scale, wanted):
    inputs = blocks[0][0][0].shape[-1]
    operands, in_specs = [], []
    count = len(blocks[0])
    used = [blocks[0]] + [blocks[n] for n in wanted]
    offsets = [offset for block in used for _, _, offset in block]
    step = 2 if all(x % 2 == 0 for x in [size, first, *offsets]) else 1
    for block in used:
        for array, stack, offset in block:
            operands.append(array)
            rows = array.shape[-2]
            at = offset // step
            lead = array.shape[:-3] if stack is None else array.shape[1:-3]
            zeros = (0,) * len(lead)
            if stack is None:
                shape = (*lead, step, rows, inputs)
                index = lambda i, j, a=at, z=zeros: (*z, a + i, 0, 0)
            else:
                shape = (None, *lead, step, rows, inputs)
                index = lambda i, j, a=at, s=stack, z=zeros: (s, *z, a + i, 0, 0)
            in_specs.append(pl.BlockSpec(shape, index))
    depth = sum(
        math.prod(x.shape[:-3] if st is None else x.shape[1:-3]) * x.shape[-2]
        for x, st, _ in blocks[0]
    )
    start = wanted[0]
    apart = wanted[1] - start if len(wanted) > 1 else 1
    if apart == 1:
        steps = 1
        out_spec = pl.BlockSpec(
            tuple(map(pl.Element, (step, 2, inputs, len(wanted) * inputs))),
            lambda i, j: (first + i * step, 0, 0, start * inputs),
        )
    else:
        steps = len(wanted)
        out_spec = pl.BlockSpec(
            (step, 2, inputs, inputs), lambda i, j: (first // step + i, 0, 0, start + apart * j)
        )
    aliases = {}
    if total is not None:
        aliases = {len(operands): 0}
        operands.append(total)
        in_specs.append(pl.BlockSpec(memory_space=pl.ANY))

    def body(*refs):
        refs = list(refs)
        if total is not None:
            refs.pop(-3)
        pairs_kernel(scale, count, step, wanted, *refs)

    return pl.pallas_call(
        body,
        grid=(size // step, steps),
        out_shape=jax.ShapeDtypeStruct((kept, 2, inputs, len(blocks) * inputs), jnp.float32),
        in_specs=in_specs,
        out_specs=out_spec,
        scratch_shapes=[pltpu.VMEM((step, 2, inputs, depth), jnp.bfloat16)],
        input_output_aliases=aliases,
        compiler_params=pltpu.CompilerParams(
            vmem_limit_bytes=32 * 1024 * 1024, dimension_semantics=("arbitrary", "arbitrary")
        ),
        cost_estimate=NO_COST,
    )(*operands)


def shifted(x, axis, by):
    devices = lax.axis_size(axis)
    return lax.ppermute(x, axis, [(i, (i + by) % devices) for i in range(devices)])


def swapped(x, axis, bit):
    devices = lax.axis_size(axis)
    return lax.ppermute(x, axis, [(i, i ^ bit) for i in range(devices)])


def after(x, *earlier):
    return lax.optimization_barrier((x, *earlier))[0]


def partners(own, axis):
    devices = lax.axis_size(axis)
    return [(own, None)] + [(shifted(own, axis, -hop), None) for hop in range(1, devices // 2 + 1)]


def tick(x, *earlier):
    x = lax.optimization_barrier((x, *earlier))[0]

    def body(x_ref, out_ref):
        out_ref[...] = x_ref[...] + 1.0

    return pl.pallas_call(
        body,
        out_shape=jax.ShapeDtypeStruct(x.shape, x.dtype),
        cost_estimate=pl.CostEstimate(
            flops=10**15, bytes_accessed=2 * x.size * 4, transcendentals=0
        ),
    )(x)


def after(x, *earlier):
    return lax.optimization_barrier((x, *earlier))[0]


class Exchange:
    def __init__(self, own, axis):
        self.own, self.axis = own, axis
        place = lax.axis_index(axis)
        self.is_far = (place & 2) == 2
        self.is_odd = (place & 1) == 1

    def y(self, *earlier):
        self.over_y = swapped(after(self.own, *earlier), self.axis, 4)

    def x(self, *earlier):
        own, over_y = lax.optimization_barrier((self.own, self.over_y, *earlier))[:2]
        self.over_x = swapped(jnp.where(self.is_far, own, over_y), self.axis, 2)

    def for_core(self, *earlier):
        own, over_x, over_y = lax.optimization_barrier(
            (self.own, self.over_x, self.over_y, *earlier)
        )[:3]
        return [jnp.where(self.is_odd, own, over_x), jnp.where(self.is_odd, over_x, over_y)]

    def core(self, *earlier):
        sent = jnp.stack(self.for_core(*earlier))
        self.over_core, self.slots = swapped(sent, self.axis, 1), (0, 1)

    over_x = over_core = None
    slots = (0, 1)

    def blocks(self):
        return [
            (self.own, None),
            (self.over_core, self.slots[0]),
            (self.over_x, None),
            (self.over_core, self.slots[1]),
            (self.over_y, None),
        ]


def core_of_both(a, b, *earlier):
    sent = jnp.stack(a.for_core(*earlier) + b.for_core(*earlier))
    a.over_core = b.over_core = swapped(sent, a.axis, 1)
    a.slots, b.slots = (0, 1), (2, 3)


def on_device(voltages, window):
    tap_count, channels = window.shape
    frames_dev = voltages.shape[2] // channels
    devices = lax.axis_size("tf")
    kept = channels // devices
    planned = devices == 4 and lax.axis_size("inp") == 8 and kept == 32
    sizes = [6, 6, 6, 6, 4, 4] if planned else [kept]
    nears = [12, 12, 8] if planned else [kept]
    count = len(sizes)
    firsts = [sum(sizes[:q]) for q in range(count)]
    near_firsts = [sum(nears[:h]) for h in range(len(nears))]
    cuts = [[(1, first, size)] for first, size in zip(near_firsts, nears)]
    for hop in range(2, devices):
        cuts += [[(hop, first, size)] for first, size in zip(firsts, sizes)]
    rest_cuts = [[(hop, 0, kept) for hop in range(1, devices)]]
    groups = frames_dev // GROUP // 2
    leading = voltages[:, :, : (tap_count - 1) * channels]
    halo = lax.ppermute(leading, "tf", [(i, i - 1) for i in range(1, devices)])
    table = pltpu.with_memory_space_constraint(jnp.asarray(dft_tables(channels)), pltpu.HBM)
    window = pltpu.with_memory_space_constraint(window, pltpu.HBM)
    me = lax.axis_index("tf").astype(jnp.int32).reshape(1)
    own_a, rest = spectra_part(
        voltages, None, window, table, me, devices, 0, groups, rest_cuts, None
    )
    rest = rest.reshape(devices - 1, kept, *rest.shape[1:])
    own_b, *pieces = spectra_part(
        voltages, halo, window, table, me, devices, groups, groups, cuts, rest
    )
    near = pieces[: len(nears)]
    far = [pieces[len(nears) + q :: count] for q in range(count)]
    scale = 1.0 / math.sqrt(frames_dev * devices)

    def run_pairs(total, q, wanted, *groups_):
        blocks = [
            [(*entry, at) for entry, (_, at) in zip(entries, groups_)]
            for entries in zip(*[g for g, _ in groups_])
        ]
        return pairs(blocks, total, firsts[q], sizes[q], kept, scale, wanted)

    if not planned:
        near = swapped(near[0], "tf", 1)
        far = jnp.stack([swapped(x, "tf", hop + 2) for hop, x in enumerate(far[0])])
        wanted = tuple(range(lax.axis_size("inp") // 2 + 1))
        return run_pairs(
            None, 0, wanted, *[(partners(x, "inp"), 0) for x in (own_a, own_b, near, far)]
        )

    def over_z(q, *earlier):
        sent = lax.optimization_barrier((*far[q], *earlier))
        return [swapped(sent[hop - 2], "tf", hop) for hop in range(2, devices)]

    near_over_z = lambda h, *earlier: swapped(after(near[h], *earlier), "tf", 1)
    exchange = lambda *parts: Exchange(jnp.concatenate(parts), "inp")
    a, b = Exchange(own_a, "inp"), Exchange(own_b, "inp")
    t = jnp.zeros((8, 128), jnp.float32)

    def chunk(q, wanted):
        h = max(i for i, first in enumerate(near_firsts) if first <= firsts[q])
        at = nears[q] if q < len(nears) else 0
        return run_pairs(
            total,
            q,
            wanted,
            (a.blocks(), firsts[q]),
            (b.blocks(), firsts[q]),
            (lines[h].blocks(), firsts[q] - near_firsts[h]),
            (lines[q].blocks(), at),
            (lines[q].blocks(), at + sizes[q]),
        )

    total = None
    a.y()
    t = tick(t, own_b[:1, :8, :128])
    z, n, lines = [over_z(0, t)], [near_over_z(0, t)], []
    b.y(t)
    a.x(t)
    t = tick(t, *z[0])
    z.append(over_z(1, t))
    n.append(near_over_z(1, n[0], t))
    lines.append(exchange(n[0], *z[0]))
    lines[0].y(b.over_y, t)
    b.x(a.over_x, t)
    t = tick(t, *z[1], b.over_y, a.over_x)
    z.append(over_z(2, t))
    n.append(near_over_z(2, n[1], t))
    lines.append(exchange(n[1], *z[1]))
    lines[1].y(lines[0].over_y, t)
    lines[0].x(b.over_x, t)
    early, late, full = (0, 4), (1, 2, 3), (0, 1, 2, 3, 4)
    t = tick(t, *z[2], lines[0].over_y, b.over_x)
    z.append(over_z(3, t))
    lines.append(exchange(n[2], *z[2]))
    lines[2].y(lines[1].over_y, t)
    lines[1].x(lines[0].over_x, t)
    core_of_both(a, b, t)
    total = chunk(0, early)
    t = tick(t, *z[3], lines[1].over_y, lines[0].over_x, total)
    z.append(over_z(4, t))
    lines.append(exchange(*z[3]))
    lines[3].y(lines[2].over_y, t)
    lines[2].x(lines[1].over_x, t)
    lines[0].core(a.over_core, t)
    total = chunk(1, early)
    t = tick(t, *z[4], lines[2].over_y, lines[1].over_x, a.over_core, total)
    z.append(over_z(5, t))
    lines.append(exchange(*z[4]))
    total = chunk(2, early)
    lines[4].y(lines[3].over_y, t, total)
    lines[3].x(lines[2].over_x, t)
    total = chunk(0, late)
    lines[1].core(lines[0].over_core, t, total)
    t = tick(t, *z[5], lines[3].over_y, lines[2].over_x, lines[0].over_core)
    lines.append(exchange(*z[5]))
    lines[5].y(lines[4].over_y, t)
    lines[4].x(lines[3].over_x, t)
    lines[2].core(lines[1].over_core, t)
    total = chunk(1, late)
    t = tick(t, lines[4].over_y, lines[3].over_x, lines[1].over_core, total)
    lines[5].x(lines[4].over_x, t)
    lines[3].core(lines[2].over_core, t)
    total = chunk(2, late)
    t = tick(t, lines[5].over_y, lines[4].over_x, lines[2].over_core, total)
    core_of_both(lines[4], lines[5], t, lines[3].over_core)
    total = chunk(3, full)
    total = chunk(4, full)
    total = chunk(5, full)
    return total


def solution(mesh):
    in_specs = (P(None, "inp", "tf"), P())
    out_specs = P("tf", None, "inp", None)
    return jax.shard_map(
        on_device, mesh=mesh, in_specs=in_specs, out_specs=out_specs, check_vma=False
    )
```
